32 devices in a mesh: rows: 4 (over y, x), pairs: 8 (over z, core).
Axes of the slice: x: 2, y: 2, z: 4, core: 2. Of those that a mesh axis runs over, the one named last changes fastest.
Arguments:
- unit_rows: float32 [4, 8, 384, 4096], P('rows', 'pairs'), may hold values from -6 to 6
- unit_counts: int32 [4, 8], P('rows'), may hold values from 1 to 384, 1024 in all within a row
- seating: int32 [16], replicated, may hold values from 0 to 15, each once
- channel_scale: float32 [4096], replicated, may hold values from 0.25 to 4
Outputs:
- rotated: float32 [4096, 4096], P('rows', 'pairs')
The draws below stay inside these ranges and needn't reach their ends.
Inputs may be any that keep to these rules, and one draw needn't show every extreme that they name: `unit_counts`: each row of 8 counts sums to 1024, and in each row the largest is exactly 384. `seating`: each block once.
All inputs are finite; a program needn't handle non-finite values.
Results may differ from the reference program's by a relative error of at most 0.0001.
Values sent between devices are 32-bit elements; how exact they have to be, the bound alone decides.
A program may use at most 128 MiB of HBM per device.

```python
import math
import jax
import jax.numpy as jnp
import numpy as np
from jax import lax

ROWS_DEV = 1024
BLOCK = 256
ROUNDS = 2
BLOCKS = 16
COLUMNS = 4096
UNIT_CAP = 384
TOTAL_ROWS = 4096
N_ROWS = 4
N_PAIRS = 8


def block_scale(rng, dims, split, smallest, high):
    def one(position, blocks):
        heights = jax.random.uniform(jax.random.fold_in(jax.random.fold_in(rng, 6), position), (blocks,), jnp.float32, smallest / len(split), high / len(split))
        return jnp.repeat(jnp.exp(heights), dims[position] // blocks).reshape((-1,) + (1,) * (len(dims) - position - 1))

    factor_of = one(*split[0])
    for cut in split[1:]:
        factor_of = factor_of * one(*cut)
    return factor_of


def split_up(number_of, total, most, lean):
    weights = [(1 << 20) // math.isqrt(grade ** lean) + 1 for grade in range(2, number_of + 1)]
    rest, given = total - most - (number_of - 1), [1] * (number_of - 1)
    while rest > 0:
        free = [i for i in range(number_of - 1) if given[i] < most]
        whole, budget = sum([weights[i] for i in free]), rest
        for i in free:
            addition = min(most - given[i], max(1, budget * weights[i] // whole), rest)
            given[i] = given[i] + addition
            rest = rest - addition
    return np.array([most] + given)


def uneven(key, amount, total, most, slope):
    if amount == 2:
        one = jax.random.randint(key, (), max(1, total - most), min(most, total - 1) + 1)
        return jnp.stack([one, total - one])
    sizes = jnp.asarray(split_up(amount, total, most, slope), jnp.int32)
    pairs = (amount - 1) // 2
    giver, taker = sizes[1:1 + 2 * pairs:2], sizes[2:2 + 2 * pairs:2]
    margin = jnp.minimum(giver - 1, most - taker)
    shifted = jax.random.randint(jax.random.fold_in(key, 1), (pairs,), 0, 1 << 20) % (margin + 1)
    sizes = sizes.at[1:1 + 2 * pairs:2].set(giver - shifted).at[2:2 + 2 * pairs:2].set(taker + shifted)
    return sizes[jax.random.permutation(jax.random.fold_in(key, 2), amount)]


def noise(stream_key, dims, spread, most, shards=(), kind=jnp.bfloat16):
    loudness = block_scale(stream_key, dims, shards, -0.22, 0.18) if shards else 1.0
    entries = jax.random.normal(stream_key, dims, jnp.float32) * spread * loudness
    return jnp.minimum(jnp.maximum(entries, -most), most).astype(kind)


def setup_inputs(seed: int = 0) -> dict:
    streams_of = jax.random.split(jax.random.key(seed), 5)
    unit_rows = noise(streams_of[0], (N_ROWS, N_PAIRS, UNIT_CAP, COLUMNS), 1.0, 6.0, ((0, 4), (1, 8)), jnp.float32)
    unit_counts = jax.vmap(lambda own: uneven(own, N_PAIRS, ROWS_DEV, UNIT_CAP, 2))(jax.random.split(streams_of[1], N_ROWS)).reshape((N_ROWS, N_PAIRS)).astype(jnp.int32)
    seating = jax.random.permutation(streams_of[2], BLOCKS).astype(jnp.int32)
    channel_scale = jnp.clip(jnp.exp(jax.random.uniform(streams_of[3], (COLUMNS,), jnp.float32, math.log(0.25), math.log(4.0))), 0.25, 4.0)
    return {"unit_rows": unit_rows, "unit_counts": unit_counts, "seating": seating, "channel_scale": channel_scale}


epsilon = 1e-06

def rotate(pair_panel):
    gram_full = lax.dot_general(pair_panel.astype(jnp.float32), pair_panel.astype(jnp.float32), (((0,), (0,)), ((), ())), precision=lax.Precision.HIGHEST, preferred_element_type=jnp.float32)
    diag_terms = jnp.diagonal(gram_full)
    skew_part = gram_full * (diag_terms[None, :] - diag_terms[:, None]) / (2.0 * (diag_terms[:, None] ** 2 + diag_terms[None, :] ** 2) + epsilon)
    skew_square = jnp.dot(skew_part, skew_part, precision=lax.Precision.HIGHEST)
    identity = jnp.eye(skew_part.shape[0], dtype=jnp.float32)
    numerator = identity + skew_part + 0.25 * skew_square
    sym_part = identity - 0.25 * skew_square
    rotation = jnp.linalg.solve(sym_part, numerator.T).T
    return jnp.dot(pair_panel, rotation, precision=lax.Precision.HIGHEST)

def advance(seated):
    upper = seated[:, 0::2]
    lower = seated[:, 1::2]
    new_upper = jnp.concatenate([upper[:, :1], lower[:, :1], upper[:, 1:-1]], axis=1)
    new_lower = jnp.concatenate([lower[:, 1:], upper[:, -1:]], axis=1)
    return jnp.stack([new_upper, new_lower], axis=2).reshape(seated.shape)

def reference(unit_rows, unit_counts, seating, channel_scale):
    flat_rows = unit_rows.reshape(N_ROWS * N_PAIRS * UNIT_CAP, COLUMNS)
    flat_counts = unit_counts.reshape(N_ROWS * N_PAIRS).astype(jnp.int32)
    unit_ends = jnp.cumsum(flat_counts).astype(jnp.int32)
    target = jnp.arange(TOTAL_ROWS, dtype=jnp.int32)
    passed = (target[:, None] >= unit_ends[None, :]).astype(jnp.int32)
    owner_unit = jnp.sum(passed, axis=1).astype(jnp.int32)
    owner_start = jnp.sum(passed * flat_counts[None, :], axis=1).astype(jnp.int32)
    source = (owner_unit * UNIT_CAP + target - owner_start).astype(jnp.int32)
    residuals = jnp.take(flat_rows, source, axis=0) * channel_scale[None, :]
    seated = jnp.take(residuals.reshape(TOTAL_ROWS, BLOCKS, BLOCK), seating.astype(jnp.int32), axis=1)
    for round_index in range(ROUNDS):
        pair_panels = seated.reshape(TOTAL_ROWS, N_PAIRS, 2 * BLOCK).transpose(1, 0, 2)
        turned = lax.map(rotate, pair_panels)
        seated = turned.transpose(1, 0, 2).reshape(TOTAL_ROWS, BLOCKS, BLOCK)
        if round_index + 1 < ROUNDS:
            seated = advance(seated)
    return seated.reshape(TOTAL_ROWS, COLUMNS)
```

```python
import functools

import jax
import jax.numpy as jnp
from jax import lax
from jax.experimental import pallas as pl
from jax.experimental.pallas import tpu as pltpu
from jax.sharding import PartitionSpec as P

ROWS_DEV = 1024
BLOCK = 256
ROUNDS = 2
WIDTH = 2 * BLOCK
TILE = 128
ALIGN = 8
MARGIN = 16
CHUNKS = 4
NEWTON_STEPS = 18
SERIES_BOUND = 1e-6
VMEM_LIMIT = 48 * 1024 * 1024

epsilon = 1e-06

MESH = pl.DeviceIdType.MESH
TILE_PAIRS = [(i, j) for i in range(WIDTH // TILE) for j in range(i, WIDTH // TILE)]
PACKED = len(TILE_PAIRS) * TILE


def halves(x):
    high = x.astype(jnp.bfloat16)
    low = (x - high.astype(jnp.float32)).astype(jnp.bfloat16)
    return high, low


def dot_halves(a, b):
    mul = functools.partial(jnp.dot, preferred_element_type=jnp.float32)
    return mul(a[0], b[0]) + (mul(a[0], b[1]) + mul(a[1], b[0]))


def dot_three(a, b):
    return dot_halves(halves(a), halves(b))


def add_gram(main, cross, block):
    high, low = halves(block)
    mul = functools.partial(
        lax.dot_general,
        dimension_numbers=(((0,), (0,)), ((), ())),
        preferred_element_type=jnp.float32,
    )
    main[...] += mul(high, high)
    cross[...] += mul(high, low)


def pack_gram(main, cross, packed):
    for t, (i, j) in enumerate(TILE_PAIRS):
        rows, cols = pl.ds(i * TILE, TILE), pl.ds(j * TILE, TILE)
        packed[pl.ds(t * TILE, TILE), :] = (
            main[rows, cols] + cross[rows, cols] + cross[cols, rows].T
        )


def remote(src, dst, send_sem, recv_sem, axis, index):
    return pltpu.make_async_remote_copy(
        src_ref=src,
        dst_ref=dst,
        send_sem=send_sem,
        recv_sem=recv_sem,
        device_id={axis: index},
        device_id_type=MESH,
    )


def signal_peers(barrier, axis, count):
    mine = lax.axis_index(axis)
    for d in range(1, count):
        pl.semaphore_signal(
            barrier,
            inc=1,
            device_id={axis: lax.rem(mine + d, count)},
            device_id_type=MESH,
        )


def sum_over_rows(count, packed, parts, total, scatter_send, scatter_recv, gather_send, gather_recv, between):
    mine = lax.axis_index("rows")
    share = PACKED // count

    def part(index):
        return pl.ds(pl.multiple_of(index * share, 8), share)

    scatter = []
    for d in range(1, count):
        peer = lax.rem(mine + d, count)
        copy = remote(packed.at[part(peer)], parts.at[d - 1], scatter_send.at[d - 1], scatter_recv.at[d - 1], "rows", peer)
        copy.start()
        scatter.append(copy)
    between()
    summed = packed[part(mine), :]
    for d in range(1, count):
        scatter[d - 1].wait_recv()
        summed = summed + parts[d - 1]
    total[part(mine), :] = summed
    gather = []
    for d in range(1, count):
        peer = lax.rem(mine + d, count)
        copy = remote(total.at[part(mine)], total.at[part(mine)], gather_send.at[d - 1], gather_recv.at[d - 1], "rows", peer)
        copy.start()
        gather.append(copy)
    for d in range(1, count):
        source = lax.rem(mine + count - d, count)
        remote(total.at[part(source)], total.at[part(source)], gather_send.at[d - 1], gather_recv.at[d - 1], "rows", source).wait_recv()
    for copy in scatter + gather:
        copy.wait_send()


def seat_kernel(pairs, seating_ref, counts_ref, unit_ref, scale_ref, out_ref):
    mine = lax.axis_index("pairs")
    start = jnp.int32(0)
    for k in range(pairs):
        start = start + jnp.where(k < mine, counts_ref[0, k], 0)
    block = unit_ref[0, 0]
    live = lax.broadcasted_iota(jnp.int32, block.shape, 0) < counts_ref[0, mine]
    scaled = jnp.where(live, block * scale_ref[...], 0.0)
    margin = jnp.zeros((out_ref.shape[1] - block.shape[0], BLOCK), jnp.float32)
    out_ref[0] = pltpu.roll(jnp.concatenate([scaled, margin], axis=0), start & (ALIGN - 1), 0)


def seat(pairs, unit_rows, channel_scale, seating, unit_counts):
    capacity, columns = unit_rows.shape[2:]
    room = capacity + MARGIN
    return pl.pallas_call(
        functools.partial(seat_kernel, pairs),
        out_shape=jax.ShapeDtypeStruct((pairs, room, WIDTH), jnp.float32),
        grid_spec=pltpu.PrefetchScalarGridSpec(
            num_scalar_prefetch=2,
            grid=(2 * pairs,),
            in_specs=[
                pl.BlockSpec((1, 1, capacity, BLOCK), lambda i, seating, counts: (0, 0, 0, seating[i])),
                pl.BlockSpec((1, BLOCK), lambda i, seating, counts: (0, seating[i])),
            ],
            out_specs=pl.BlockSpec((1, room, BLOCK), lambda i, seating, counts: (i // 2, 0, i % 2)),
        ),
        compiler_params=pltpu.CompilerParams(vmem_limit_bytes=VMEM_LIMIT),
        name="seat",
    )(seating, unit_counts, unit_rows, channel_scale)


def collect_kernel(
    pairs, rows, room,
    seated, units_ref, gram_ref,
    landed, main, cross, packed, parts, total,
    send_sem, recv_sem, keep_sem, out_sem, scatter_send, scatter_recv, gather_send, gather_recv,
):
    mine = lax.axis_index("pairs")
    barrier = pltpu.get_barrier_semaphore()
    signal_peers(barrier, "pairs", pairs)
    signal_peers(barrier, "rows", rows)
    keep = pltpu.make_async_copy(seated.at[mine], landed.at[mine], keep_sem)
    keep.start()
    main[...] = jnp.zeros_like(main)
    cross[...] = jnp.zeros_like(cross)
    pl.semaphore_wait(barrier, pairs + rows - 2)

    def copy_to(d):
        peer = lax.rem(mine + d, pairs)
        return remote(seated.at[peer], landed.at[mine], send_sem.at[d - 1], recv_sem.at[d - 1], "pairs", peer)

    def write_out(source, d):
        return pltpu.make_async_copy(landed.at[source], units_ref.at[source], out_sem.at[d])

    def send(d, carry):
        copy_to(d).start()
        return carry

    lax.fori_loop(1, pairs, send, 0)
    keep.wait()
    write_out(mine, 0).start()
    add_gram(main, cross, landed[mine])

    def receive(d, carry):
        source = lax.rem(mine + pairs - d, pairs)
        remote(seated.at[source], landed.at[source], send_sem.at[d - 1], recv_sem.at[d - 1], "pairs", source).wait_recv()
        write_out(source, d).start()
        add_gram(main, cross, landed[source])
        return carry

    lax.fori_loop(1, pairs, receive, 0)
    pack_gram(main, cross, packed)
    sum_over_rows(rows, packed, parts, total, scatter_send, scatter_recv, gather_send, gather_recv, lambda: None)
    gram_ref[...] = total[...]
    write_out(mine, 0).wait()

    def finish(d, carry):
        copy_to(d).wait_send()
        write_out(lax.rem(mine + pairs - d, pairs), d).wait()
        return carry

    lax.fori_loop(1, pairs, finish, 0)


def gram_scratch(rows):
    return [
        pltpu.VMEM((WIDTH, WIDTH), jnp.float32),
        pltpu.VMEM((WIDTH, WIDTH), jnp.float32),
        pltpu.VMEM((PACKED, TILE), jnp.float32),
        pltpu.VMEM((rows - 1, PACKED // rows, TILE), jnp.float32),
        pltpu.VMEM((PACKED, TILE), jnp.float32),
    ]


def row_sems(rows):
    return [pltpu.SemaphoreType.DMA((rows - 1,))] * 4


ANY_SPEC = pl.BlockSpec(memory_space=pl.ANY)
VMEM_SPEC = pl.BlockSpec(memory_space=pltpu.VMEM)
SMEM_SPEC = pl.BlockSpec(memory_space=pltpu.SMEM)
PANEL_AND_GRAM = (
    jax.ShapeDtypeStruct((ROWS_DEV, WIDTH), jnp.float32),
    jax.ShapeDtypeStruct((PACKED, TILE), jnp.float32),
)


def collect(pairs, rows, seated):
    return pl.pallas_call(
        functools.partial(collect_kernel, pairs, rows, seated.shape[1]),
        out_shape=(
            jax.ShapeDtypeStruct(seated.shape, jnp.float32),
            jax.ShapeDtypeStruct((PACKED, TILE), jnp.float32),
        ),
        in_specs=[ANY_SPEC],
        out_specs=(ANY_SPEC, VMEM_SPEC),
        scratch_shapes=[
            pltpu.VMEM(seated.shape, jnp.float32),
            *gram_scratch(rows),
            pltpu.SemaphoreType.DMA((pairs - 1,)),
            pltpu.SemaphoreType.DMA((pairs - 1,)),
            pltpu.SemaphoreType.DMA,
            pltpu.SemaphoreType.DMA((pairs,)),
            *row_sems(rows),
        ],
        compiler_params=pltpu.CompilerParams(
            collective_id=0, has_side_effects=True, vmem_limit_bytes=VMEM_LIMIT
        ),
        name="collect",
    )(seated)


def exchange_kernel(
    pairs, rows,
    old_ref, panel_ref, gram_ref,
    landed, main, cross, packed, parts, total,
    up_send, up_recv, down_send, down_recv, scatter_send, scatter_recv, gather_send, gather_recv,
):
    mine = lax.axis_index("pairs")
    last = pairs - 1
    barrier = pltpu.get_barrier_semaphore()
    signal_peers(barrier, "rows", rows)

    def greet(index):
        pl.semaphore_signal(barrier, inc=1, device_id={"pairs": index}, device_id_type=MESH)

    @pl.when(mine < last)
    def _():
        greet(mine + 1)

    @pl.when(mine > 0)
    def _():
        greet(mine - 1)

    main[...] = jnp.zeros_like(main)
    cross[...] = jnp.zeros_like(cross)
    greeted = jnp.where(mine < last, 1, 0) + jnp.where(mine > 0, 1, 0)
    pl.semaphore_wait(barrier, rows - 1 + greeted)

    size = ROWS_DEV // CHUNKS
    upper, lower = pl.ds(0, BLOCK), pl.ds(BLOCK, BLOCK)

    def up(c, source):
        here = pl.ds(c * size, size)
        return remote(old_ref.at[here, source], landed.at[here, upper], up_send.at[c], up_recv.at[c], "pairs", mine + 1)

    def down(c):
        here = pl.ds(c * size, size)
        return remote(old_ref.at[here, lower], landed.at[here, lower], down_send.at[c], down_recv.at[c], "pairs", mine - 1)

    for c in range(CHUNKS):
        @pl.when(mine == 0)
        def _():
            up(c, lower).start()

        @pl.when((mine > 0) & (mine < last))
        def _():
            up(c, upper).start()

        @pl.when(mine > 0)
        def _():
            down(c).start()

    @pl.when(mine == 0)
    def _():
        landed[:, upper] = old_ref[:, upper]

    @pl.when(mine == last)
    def _():
        landed[:, lower] = old_ref[:, upper]

    for c in range(CHUNKS):
        @pl.when(mine > 0)
        def _():
            up(c, upper).wait_recv()

        @pl.when(mine < last)
        def _():
            down(c).wait_recv()

        add_gram(main, cross, landed[pl.ds(c * size, size), :])
    pack_gram(main, cross, packed)

    def hand_over():
        panel_ref[...] = landed[...]

    sum_over_rows(rows, packed, parts, total, scatter_send, scatter_recv, gather_send, gather_recv, hand_over)
    gram_ref[...] = total[...]
    for c in range(CHUNKS):
        @pl.when(mine < last)
        def _():
            up(c, upper).wait_send()

        @pl.when(mine > 0)
        def _():
            down(c).wait_send()


def exchange(pairs, rows, panel):
    return pl.pallas_call(
        functools.partial(exchange_kernel, pairs, rows),
        out_shape=PANEL_AND_GRAM,
        in_specs=[VMEM_SPEC],
        out_specs=(VMEM_SPEC, VMEM_SPEC),
        scratch_shapes=[
            pltpu.VMEM((ROWS_DEV, WIDTH), jnp.float32),
            *gram_scratch(rows),
            *[pltpu.SemaphoreType.DMA((CHUNKS,))] * 4,
            *row_sems(rows),
        ],
        compiler_params=pltpu.CompilerParams(
            collective_id=1, has_side_effects=True, vmem_limit_bytes=VMEM_LIMIT
        ),
        name="exchange",
    )(panel)


def turn_units_kernel(counts_ref, packed, units_ref, out, units, panel, load_sem, *scratch):
    pairs, room = units.shape[:2]
    load = pltpu.make_async_copy(units_ref, units, load_sem)
    load.start()

    def compact():
        load.wait()
        start = jnp.int32(0)
        head = lax.broadcasted_iota(jnp.int32, (ALIGN, WIDTH), 0)
        for k in range(pairs):
            first = pl.multiple_of(start & -ALIGN, ALIGN)
            top = pl.ds(first, ALIGN)
            panel[top, :] = jnp.where(head < (start & (ALIGN - 1)), panel[top, :], units[k, pl.ds(0, ALIGN), :])
            panel[pl.ds(pl.multiple_of(first + ALIGN, ALIGN), room - ALIGN), :] = units[k, pl.ds(ALIGN, room - ALIGN), :]
            start = start + counts_ref[0, k]

    turn_panel(packed, panel, out, compact, *scratch)


def turn_kernel(packed, panel, out, *scratch):
    turn_panel(packed, panel, out, lambda: None, *scratch)


def turn_panel(packed, panel, out, prepare, gram, tangent, square, change):
    on_diag = lax.broadcasted_iota(jnp.int32, (TILE, TILE), 0) == lax.broadcasted_iota(jnp.int32, (TILE, TILE), 1)
    across, along = [], []
    for t, (i, j) in enumerate(TILE_PAIRS):
        tile = packed[pl.ds(t * TILE, TILE), :]
        gram[pl.ds(i * TILE, TILE), pl.ds(j * TILE, TILE)] = tile
        if i == j:
            kept = jnp.where(on_diag, tile, 0.0)
            across.append(jnp.sum(kept, axis=0, keepdims=True))
            along.append(jnp.sum(kept, axis=1, keepdims=True))
        else:
            gram[pl.ds(j * TILE, TILE), pl.ds(i * TILE, TILE)] = tile.T
    diag_row = jnp.concatenate(across, axis=1)
    diag_col = jnp.concatenate(along, axis=0)
    tangent[...] = 0.5 * (
        gram[...] * (diag_row - diag_col) / (2.0 * (diag_col**2 + diag_row**2) + epsilon)
    )
    t_halves = halves(tangent[...])
    square[...] = dot_halves(t_halves, t_halves)
    m_halves = halves(square[...])
    fourth = dot_halves(m_halves, m_halves)
    rest = jnp.sum(fourth * fourth)
    short = rest <= SERIES_BOUND

    @pl.when(short)
    def _():
        first = tangent[...] + square[...]
        second = first + dot_halves(halves(first), m_halves)
        change[...] = 2.0 * (second + dot_three(second, fourth))

    @pl.when(jnp.logical_not(short))
    def _():
        exact = functools.partial(
            jnp.dot, precision=lax.Precision.HIGHEST, preferred_element_type=jnp.float32
        )
        eye = (
            lax.broadcasted_iota(jnp.int32, (WIDTH, WIDTH), 0)
            == lax.broadcasted_iota(jnp.int32, (WIDTH, WIDTH), 1)
        )
        square[...] = exact(tangent[...], tangent[...])
        bound = jnp.sqrt(jnp.sqrt(jnp.full((1, 1), rest, jnp.float32))) * 1.01
        change[...] = jnp.where(eye, 2.0 / (2.0 + bound), 0.0)

        def newton(step, carry):
            inverse = change[...]
            residual = jnp.where(eye, 1.0, 0.0) - inverse + exact(square[...], inverse)
            change[...] = inverse + exact(inverse, residual)
            return carry

        lax.fori_loop(0, NEWTON_STEPS, newton, 0)
        change[...] = 2.0 * exact(tangent[...] + square[...], change[...])

    prepare()
    d_halves = halves(change[...])
    size = ROWS_DEV // CHUNKS

    def apply(c, carry):
        here = pl.ds(pl.multiple_of(c * size, size), size)
        block = panel[here, :]
        out[here, :] = block + dot_halves(halves(block), d_halves)
        return carry

    lax.fori_loop(0, CHUNKS, apply, 0)


def turn_units(unit_counts, packed, units):
    pairs, room = units.shape[:2]
    return pl.pallas_call(
        turn_units_kernel,
        out_shape=PANEL_AND_GRAM[0],
        in_specs=[SMEM_SPEC, VMEM_SPEC, ANY_SPEC],
        out_specs=VMEM_SPEC,
        scratch_shapes=[
            pltpu.VMEM(units.shape, jnp.float32),
            pltpu.VMEM((ROWS_DEV + room, WIDTH), jnp.float32),
            pltpu.SemaphoreType.DMA,
            *[pltpu.VMEM((WIDTH, WIDTH), jnp.float32)] * 4,
        ],
        compiler_params=pltpu.CompilerParams(vmem_limit_bytes=VMEM_LIMIT),
        name="turn_units",
    )(unit_counts, packed, units)


def turn(packed, panel):
    return pl.pallas_call(
        turn_kernel,
        out_shape=PANEL_AND_GRAM[0],
        in_specs=[VMEM_SPEC, VMEM_SPEC],
        out_specs=VMEM_SPEC,
        scratch_shapes=[pltpu.VMEM((WIDTH, WIDTH), jnp.float32)] * 4,
        compiler_params=pltpu.CompilerParams(vmem_limit_bytes=VMEM_LIMIT),
        name="turn",
    )(packed, panel)


def local(pairs, rows, unit_rows, unit_counts, seating, channel_scale):
    seated = seat(pairs, unit_rows, channel_scale[None, :], seating, unit_counts)
    units, gram = collect(pairs, rows, seated)
    panel = turn_units(unit_counts, gram, units)
    for round_index in range(1, ROUNDS):
        panel, gram = exchange(pairs, rows, panel)
        panel = turn(gram, panel)
    return panel


def solution(mesh):
    return jax.shard_map(
        functools.partial(local, mesh.shape["pairs"], mesh.shape["rows"]),
        mesh=mesh,
        in_specs=(P("rows", "pairs", None, None), P("rows", None), P(), P()),
        out_specs=P("rows", "pairs"),
        check_vma=False,
    )
```

```python
import functools

import jax
import jax.numpy as jnp
from jax import lax
from jax.experimental import pallas as pl
from jax.experimental.pallas import tpu as pltpu
from jax.sharding import PartitionSpec as P

ROWS_DEV = 1024
BLOCK = 256
ROUNDS = 2
WIDTH = 2 * BLOCK
TILE = 128
ALIGN = 8
BAND = 64
CHUNKS = 4
NEWTON_STEPS = 18
SERIES_BOUND = 1e-6
VMEM_LIMIT = 48 * 1024 * 1024

epsilon = 1e-06

MESH = pl.DeviceIdType.MESH
TILE_PAIRS = [(i, j) for i in range(WIDTH // TILE) for j in range(i, WIDTH // TILE)]
PACKED = len(TILE_PAIRS) * TILE


def halves(x):
    high = x.astype(jnp.bfloat16)
    low = (x - high.astype(jnp.float32)).astype(jnp.bfloat16)
    return high, low


def dot_halves(a, b):
    mul = functools.partial(jnp.dot, preferred_element_type=jnp.float32)
    return mul(a[0], b[0]) + (mul(a[0], b[1]) + mul(a[1], b[0]))


def dot_once(a, b):
    return jnp.dot(a.astype(jnp.bfloat16), b.astype(jnp.bfloat16), preferred_element_type=jnp.float32)


def add_gram(main, cross, block):
    high, low = halves(block)
    mul = functools.partial(
        lax.dot_general,
        dimension_numbers=(((0,), (0,)), ((), ())),
        preferred_element_type=jnp.float32,
    )
    main[...] += mul(high, high)
    cross[...] += mul(high, low)


def pack_gram(main, cross, packed):
    for t, (i, j) in enumerate(TILE_PAIRS):
        rows, cols = pl.ds(i * TILE, TILE), pl.ds(j * TILE, TILE)
        packed[pl.ds(t * TILE, TILE), :] = (
            main[rows, cols] + cross[rows, cols] + cross[cols, rows].T
        )


def remote(src, dst, send_sem, recv_sem, axis, index):
    return pltpu.make_async_remote_copy(
        src_ref=src,
        dst_ref=dst,
        send_sem=send_sem,
        recv_sem=recv_sem,
        device_id={axis: index},
        device_id_type=MESH,
    )


def signal_peers(barrier, axis, count):
    mine = lax.axis_index(axis)
    for d in range(1, count):
        pl.semaphore_signal(
            barrier,
            inc=1,
            device_id={axis: lax.rem(mine + d, count)},
            device_id_type=MESH,
        )


def sum_over_rows(count, packed, parts, total, scatter_send, scatter_recv, gather_send, gather_recv, between):
    mine = lax.axis_index("rows")
    share = PACKED // count

    def part(index):
        return pl.ds(pl.multiple_of(index * share, 8), share)

    scatter = []
    for d in range(1, count):
        peer = lax.rem(mine + d, count)
        copy = remote(packed.at[part(peer)], parts.at[d - 1], scatter_send.at[d - 1], scatter_recv.at[d - 1], "rows", peer)
        copy.start()
        scatter.append(copy)
    between()
    summed = packed[part(mine), :]
    for d in range(1, count):
        scatter[d - 1].wait_recv()
        summed = summed + parts[d - 1]
    total[part(mine), :] = summed
    gather = []
    for d in range(1, count):
        peer = lax.rem(mine + d, count)
        copy = remote(total.at[part(mine)], total.at[part(mine)], gather_send.at[d - 1], gather_recv.at[d - 1], "rows", peer)
        copy.start()
        gather.append(copy)
    for d in range(1, count):
        source = lax.rem(mine + count - d, count)
        remote(total.at[part(source)], total.at[part(source)], gather_send.at[d - 1], gather_recv.at[d - 1], "rows", source).wait_recv()
    for copy in scatter + gather:
        copy.wait_send()


def collect_kernel(
    pairs, rows, room,
    unit_ref, scale_ref, seating_ref, counts_ref, units_ref, gram_ref,
    unit, seated, landed, main, cross, packed, parts, total,
    send_sem, recv_sem, load_sem, out_sem, scatter_send, scatter_recv, gather_send, gather_recv,
):
    mine = lax.axis_index("pairs")
    barrier = pltpu.get_barrier_semaphore()
    signal_peers(barrier, "pairs", pairs)
    signal_peers(barrier, "rows", rows)
    load = pltpu.make_async_copy(unit_ref.at[0, 0], unit, load_sem)
    load.start()
    main[...] = jnp.zeros_like(main)
    cross[...] = jnp.zeros_like(cross)
    band_row = lax.broadcasted_iota(jnp.int32, (BAND, BLOCK), 0)
    own_count = counts_ref[0, mine]
    load.wait()
    pl.semaphore_wait(barrier, pairs + rows - 2)

    blocks = unit.shape[1] // BLOCK

    def choose(ref, rows, seat):
        chosen = ref[rows, pl.ds(0, BLOCK)]
        at = jnp.broadcast_to(seat, chosen.shape)
        for index in range(1, blocks):
            chosen = jnp.where(at == index, ref[rows, pl.ds(index * BLOCK, BLOCK)], chosen)
        return chosen

    def fill(block, pair):
        for h in range(2):
            seat = seating_ref[2 * pair + h]
            scale = choose(scale_ref, pl.ds(0, 1), seat)

            def part(i, carry):
                rows = pl.ds(pl.multiple_of(i * BAND, BAND), BAND)
                live = band_row + i * BAND < own_count
                block[rows, pl.ds(h * BLOCK, BLOCK)] = jnp.where(live, choose(unit, rows, seat) * scale, 0.0)
                return carry

            lax.fori_loop(0, room // BAND, part, 0)

    def copy_to(d):
        peer = lax.rem(mine + d, pairs)
        return remote(seated.at[d - 1], landed.at[mine], send_sem.at[d - 1], recv_sem.at[d - 1], "pairs", peer)

    def write_out(source, d):
        return pltpu.make_async_copy(landed.at[source], units_ref.at[source], out_sem.at[d])

    def send(d, carry):
        fill(seated.at[d - 1], lax.rem(mine + d, pairs))
        copy_to(d).start()
        return carry

    lax.fori_loop(1, pairs, send, 0)
    fill(landed.at[mine], mine)
    write_out(mine, 0).start()
    add_gram(main, cross, landed[mine])

    def receive(d, carry):
        source = lax.rem(mine + pairs - d, pairs)
        remote(seated.at[d - 1], landed.at[source], send_sem.at[d - 1], recv_sem.at[d - 1], "pairs", source).wait_recv()
        write_out(source, d).start()
        add_gram(main, cross, landed[source])
        return carry

    lax.fori_loop(1, pairs, receive, 0)
    pack_gram(main, cross, packed)
    sum_over_rows(rows, packed, parts, total, scatter_send, scatter_recv, gather_send, gather_recv, lambda: None)
    gram_ref[...] = total[...]
    write_out(mine, 0).wait()

    def finish(d, carry):
        copy_to(d).wait_send()
        write_out(lax.rem(mine + pairs - d, pairs), d).wait()
        return carry

    lax.fori_loop(1, pairs, finish, 0)


def gram_scratch(rows):
    return [
        pltpu.VMEM((WIDTH, WIDTH), jnp.float32),
        pltpu.VMEM((WIDTH, WIDTH), jnp.float32),
        pltpu.VMEM((PACKED, TILE), jnp.float32),
        pltpu.VMEM((rows - 1, PACKED // rows, TILE), jnp.float32),
        pltpu.VMEM((PACKED, TILE), jnp.float32),
    ]


def row_sems(rows):
    return [pltpu.SemaphoreType.DMA((rows - 1,))] * 4


ANY_SPEC = pl.BlockSpec(memory_space=pl.ANY)
VMEM_SPEC = pl.BlockSpec(memory_space=pltpu.VMEM)
SMEM_SPEC = pl.BlockSpec(memory_space=pltpu.SMEM)
PANEL_AND_GRAM = (
    jax.ShapeDtypeStruct((ROWS_DEV, WIDTH), jnp.float32),
    jax.ShapeDtypeStruct((PACKED, TILE), jnp.float32),
)


def collect(pairs, rows, unit_rows, channel_scale, seating, unit_counts):
    capacity, columns = unit_rows.shape[2:]
    units = (pairs, capacity, WIDTH)
    return pl.pallas_call(
        functools.partial(collect_kernel, pairs, rows, capacity),
        out_shape=(
            jax.ShapeDtypeStruct(units, jnp.float32),
            jax.ShapeDtypeStruct((PACKED, TILE), jnp.float32),
        ),
        in_specs=[ANY_SPEC, VMEM_SPEC, SMEM_SPEC, SMEM_SPEC],
        out_specs=(ANY_SPEC, VMEM_SPEC),
        scratch_shapes=[
            pltpu.VMEM((capacity, columns), jnp.float32),
            pltpu.VMEM((pairs - 1, capacity, WIDTH), jnp.float32),
            pltpu.VMEM(units, jnp.float32),
            *gram_scratch(rows),
            pltpu.SemaphoreType.DMA((pairs - 1,)),
            pltpu.SemaphoreType.DMA((pairs - 1,)),
            pltpu.SemaphoreType.DMA,
            pltpu.SemaphoreType.DMA((pairs,)),
            *row_sems(rows),
        ],
        compiler_params=pltpu.CompilerParams(
            collective_id=0, has_side_effects=True, vmem_limit_bytes=VMEM_LIMIT
        ),
        name="collect",
    )(unit_rows, channel_scale, seating, unit_counts)


def exchange_kernel(
    pairs, rows,
    old_ref, panel_ref, gram_ref,
    landed, main, cross, packed, parts, total,
    up_send, up_recv, down_send, down_recv, scatter_send, scatter_recv, gather_send, gather_recv,
):
    mine = lax.axis_index("pairs")
    last = pairs - 1
    barrier = pltpu.get_barrier_semaphore()
    signal_peers(barrier, "rows", rows)

    def greet(index):
        pl.semaphore_signal(barrier, inc=1, device_id={"pairs": index}, device_id_type=MESH)

    @pl.when(mine < last)
    def _():
        greet(mine + 1)

    @pl.when(mine > 0)
    def _():
        greet(mine - 1)

    main[...] = jnp.zeros_like(main)
    cross[...] = jnp.zeros_like(cross)
    greeted = jnp.where(mine < last, 1, 0) + jnp.where(mine > 0, 1, 0)
    pl.semaphore_wait(barrier, rows - 1 + greeted)

    size = ROWS_DEV // CHUNKS
    upper, lower = pl.ds(0, BLOCK), pl.ds(BLOCK, BLOCK)

    def up(c, source):
        here = pl.ds(c * size, size)
        return remote(old_ref.at[here, source], landed.at[here, upper], up_send.at[c], up_recv.at[c], "pairs", mine + 1)

    def down(c):
        here = pl.ds(c * size, size)
        return remote(old_ref.at[here, lower], landed.at[here, lower], down_send.at[c], down_recv.at[c], "pairs", mine - 1)

    for c in range(CHUNKS):
        @pl.when(mine == 0)
        def _():
            up(c, lower).start()

        @pl.when((mine > 0) & (mine < last))
        def _():
            up(c, upper).start()

        @pl.when(mine > 0)
        def _():
            down(c).start()

    @pl.when(mine == 0)
    def _():
        landed[:, upper] = old_ref[:, upper]

    @pl.when(mine == last)
    def _():
        landed[:, lower] = old_ref[:, upper]

    for c in range(CHUNKS):
        @pl.when(mine > 0)
        def _():
            up(c, upper).wait_recv()

        @pl.when(mine < last)
        def _():
            down(c).wait_recv()

        add_gram(main, cross, landed[pl.ds(c * size, size), :])
    pack_gram(main, cross, packed)

    def hand_over():
        panel_ref[...] = landed[...]

    sum_over_rows(rows, packed, parts, total, scatter_send, scatter_recv, gather_send, gather_recv, hand_over)
    gram_ref[...] = total[...]
    for c in range(CHUNKS):
        @pl.when(mine < last)
        def _():
            up(c, upper).wait_send()

        @pl.when(mine > 0)
        def _():
            down(c).wait_send()


def exchange(pairs, rows, panel):
    return pl.pallas_call(
        functools.partial(exchange_kernel, pairs, rows),
        out_shape=PANEL_AND_GRAM,
        in_specs=[VMEM_SPEC],
        out_specs=(VMEM_SPEC, VMEM_SPEC),
        scratch_shapes=[
            pltpu.VMEM((ROWS_DEV, WIDTH), jnp.float32),
            *gram_scratch(rows),
            *[pltpu.SemaphoreType.DMA((CHUNKS,))] * 4,
            *row_sems(rows),
        ],
        compiler_params=pltpu.CompilerParams(
            collective_id=1, has_side_effects=True, vmem_limit_bytes=VMEM_LIMIT
        ),
        name="exchange",
    )(panel)


def turn_units_kernel(counts_ref, packed, units_ref, out, units, panel, load_sem, *scratch):
    pairs, room = units.shape[:2]
    load = pltpu.make_async_copy(units_ref, units, load_sem)
    load.start()

    def compact():
        load.wait()
        start = jnp.int32(0)
        groups = room // ALIGN
        lane_row = lax.broadcasted_iota(jnp.int32, (groups + 1, ALIGN, WIDTH), 1)
        for k in range(pairs):
            first = pl.multiple_of(start & -ALIGN, ALIGN)
            shift = start & (ALIGN - 1)
            turned = pltpu.roll(units[k].reshape(groups, ALIGN, WIDTH), shift, 1)
            before = panel[pl.ds(first, ALIGN), :].reshape(1, ALIGN, WIDTH)
            shifted = jnp.where(
                lane_row < shift,
                jnp.concatenate([before, turned], axis=0),
                jnp.concatenate([turned, turned[-1:]], axis=0),
            )
            panel[pl.ds(first, room + ALIGN), :] = shifted.reshape(room + ALIGN, WIDTH)
            start = start + counts_ref[0, k]

    turn_panel(packed, panel, out, compact, *scratch)


def turn_kernel(packed, panel, out, *scratch):
    turn_panel(packed, panel, out, lambda: None, *scratch)


def turn_panel(packed, panel, out, prepare, gram, tangent, square, change):
    on_diag = lax.broadcasted_iota(jnp.int32, (TILE, TILE), 0) == lax.broadcasted_iota(jnp.int32, (TILE, TILE), 1)
    across, along = [], []
    for t, (i, j) in enumerate(TILE_PAIRS):
        tile = packed[pl.ds(t * TILE, TILE), :]
        gram[pl.ds(i * TILE, TILE), pl.ds(j * TILE, TILE)] = tile
        if i == j:
            kept = jnp.where(on_diag, tile, 0.0)
            across.append(jnp.sum(kept, axis=0, keepdims=True))
            along.append(jnp.sum(kept, axis=1, keepdims=True))
        else:
            gram[pl.ds(j * TILE, TILE), pl.ds(i * TILE, TILE)] = tile.T
    diag_row = jnp.concatenate(across, axis=1)
    diag_col = jnp.concatenate(along, axis=0)
    tangent[...] = 0.5 * (
        gram[...] * (diag_row - diag_col) / (2.0 * (diag_col**2 + diag_row**2) + epsilon)
    )
    t_halves = halves(tangent[...])
    square[...] = dot_halves(t_halves, t_halves)
    m_high = square[...].astype(jnp.bfloat16)
    fourth = dot_once(m_high, m_high)
    rest = jnp.sum(fourth * fourth)
    short = rest <= SERIES_BOUND

    @pl.when(short)
    def _():
        first = tangent[...] + square[...]
        second = first + dot_once(first, m_high)
        change[...] = 2.0 * (second + dot_once(second, fourth))

    @pl.when(jnp.logical_not(short))
    def _():
        exact = functools.partial(
            jnp.dot, precision=lax.Precision.HIGHEST, preferred_element_type=jnp.float32
        )
        eye = (
            lax.broadcasted_iota(jnp.int32, (WIDTH, WIDTH), 0)
            == lax.broadcasted_iota(jnp.int32, (WIDTH, WIDTH), 1)
        )
        square[...] = exact(tangent[...], tangent[...])
        bound = jnp.sqrt(jnp.sqrt(jnp.full((1, 1), rest, jnp.float32))) * 1.01
        change[...] = jnp.where(eye, 2.0 / (2.0 + bound), 0.0)

        def newton(step, carry):
            inverse = change[...]
            residual = jnp.where(eye, 1.0, 0.0) - inverse + exact(square[...], inverse)
            change[...] = inverse + exact(inverse, residual)
            return carry

        lax.fori_loop(0, NEWTON_STEPS, newton, 0)
        change[...] = 2.0 * exact(tangent[...] + square[...], change[...])

    prepare()
    d_halves = halves(change[...])
    size = ROWS_DEV // CHUNKS

    def apply(c, carry):
        here = pl.ds(pl.multiple_of(c * size, size), size)
        block = panel[here, :]
        out[here, :] = block + dot_halves(halves(block), d_halves)
        return carry

    lax.fori_loop(0, CHUNKS, apply, 0)


def turn_units(unit_counts, packed, units):
    pairs, room = units.shape[:2]
    return pl.pallas_call(
        turn_units_kernel,
        out_shape=PANEL_AND_GRAM[0],
        in_specs=[SMEM_SPEC, VMEM_SPEC, ANY_SPEC],
        out_specs=VMEM_SPEC,
        scratch_shapes=[
            pltpu.VMEM(units.shape, jnp.float32),
            pltpu.VMEM((ROWS_DEV + room + ALIGN, WIDTH), jnp.float32),
            pltpu.SemaphoreType.DMA,
            *[pltpu.VMEM((WIDTH, WIDTH), jnp.float32)] * 4,
        ],
        compiler_params=pltpu.CompilerParams(vmem_limit_bytes=VMEM_LIMIT),
        name="turn_units",
    )(unit_counts, packed, units)


def turn(packed, panel):
    return pl.pallas_call(
        turn_kernel,
        out_shape=PANEL_AND_GRAM[0],
        in_specs=[VMEM_SPEC, VMEM_SPEC],
        out_specs=VMEM_SPEC,
        scratch_shapes=[pltpu.VMEM((WIDTH, WIDTH), jnp.float32)] * 4,
        compiler_params=pltpu.CompilerParams(vmem_limit_bytes=VMEM_LIMIT),
        name="turn",
    )(packed, panel)


def local(pairs, rows, unit_rows, unit_counts, seating, channel_scale):
    units, gram = collect(pairs, rows, unit_rows, channel_scale[None, :], seating, unit_counts)
    panel = turn_units(unit_counts, gram, units)
    for round_index in range(1, ROUNDS):
        panel, gram = exchange(pairs, rows, panel)
        panel = turn(gram, panel)
    return panel


def solution(mesh):
    return jax.shard_map(
        functools.partial(local, mesh.shape["pairs"], mesh.shape["rows"]),
        mesh=mesh,
        in_specs=(P("rows", "pairs", None, None), P("rows", None), P(), P()),
        out_specs=P("rows", "pairs"),
        check_vma=False,
    )
```

```python
import functools

import jax
import jax.numpy as jnp
from jax import lax
from jax.experimental import pallas as pl
from jax.experimental.pallas import tpu as pltpu
from jax.sharding import PartitionSpec as P

ROWS_DEV = 1024
BLOCK = 256
ROUNDS = 2
WIDTH = 2 * BLOCK
TILE = 128
ALIGN = 8
BAND = 64
CHUNKS = 4
NEWTON_STEPS = 18
SERIES_BOUND = 1e-6
VMEM_LIMIT = 48 * 1024 * 1024

epsilon = 1e-06

MESH = pl.DeviceIdType.MESH
TILES = WIDTH // TILE
OFF_DIAGONAL = [(i, j) for i in range(TILES) for j in range(i + 1, TILES)]
DIAGONAL_AT = len(OFF_DIAGONAL) * TILE
EXTRA_AT = DIAGONAL_AT + TILES // 2 * TILE
EXTRA = 64
PACKED = EXTRA_AT + EXTRA


def halves(x):
    high = x.astype(jnp.bfloat16)
    low = (x - high.astype(jnp.float32)).astype(jnp.bfloat16)
    return high, low


def dot_halves(a, b):
    mul = functools.partial(jnp.dot, preferred_element_type=jnp.float32)
    return mul(a[0], b[0]) + (mul(a[0], b[1]) + mul(a[1], b[0]))


def dot_once(a, b):
    return jnp.dot(a.astype(jnp.bfloat16), b.astype(jnp.bfloat16), preferred_element_type=jnp.float32)


def add_gram(main, cross, block):
    high, low = halves(block)
    mul = functools.partial(
        lax.dot_general,
        dimension_numbers=(((0,), (0,)), ((), ())),
        preferred_element_type=jnp.float32,
    )
    main[...] += mul(high, high)
    cross[...] += mul(high, low)


def tile_iotas():
    shape = (TILE, TILE)
    return lax.broadcasted_iota(jnp.int32, shape, 0), lax.broadcasted_iota(jnp.int32, shape, 1)


def pack_gram(main, cross, packed):
    def tile(i, j):
        rows, cols = pl.ds(i * TILE, TILE), pl.ds(j * TILE, TILE)
        return main[rows, cols] + cross[rows, cols] + cross[cols, rows].T

    row, col = tile_iotas()
    for t, (i, j) in enumerate(OFF_DIAGONAL):
        packed[pl.ds(t * TILE, TILE), :] = tile(i, j)
    packed[pl.ds(EXTRA_AT, EXTRA), :] = jnp.zeros((EXTRA, TILE), jnp.float32)
    for t in range(TILES // 2):
        lower = tile(2 * t + 1, 2 * t + 1)
        packed[pl.ds(DIAGONAL_AT + t * TILE, TILE), :] = jnp.where(row <= col, tile(2 * t, 2 * t), lower)
        packed[pl.ds(EXTRA_AT + t, 1), :] = jnp.sum(jnp.where(row == col, lower, 0.0), axis=0, keepdims=True)


def unpack_gram(packed, gram):
    row, col = tile_iotas()
    across, along = [], []
    for t, (i, j) in enumerate(OFF_DIAGONAL):
        tile = packed[pl.ds(t * TILE, TILE), :]
        gram[pl.ds(i * TILE, TILE), pl.ds(j * TILE, TILE)] = tile
        gram[pl.ds(j * TILE, TILE), pl.ds(i * TILE, TILE)] = tile.T
    for t in range(TILES // 2):
        both = packed[pl.ds(DIAGONAL_AT + t * TILE, TILE), :]
        flipped = both.T
        upper = jnp.where(row <= col, both, flipped)
        lower = jnp.where(row > col, both, flipped)
        lower = jnp.where(row == col, packed[pl.ds(EXTRA_AT + t, 1), :], lower)
        for i, tile in ((2 * t, upper), (2 * t + 1, lower)):
            gram[pl.ds(i * TILE, TILE), pl.ds(i * TILE, TILE)] = tile
            kept = jnp.where(row == col, tile, 0.0)
            across.append(jnp.sum(kept, axis=0, keepdims=True))
            along.append(jnp.sum(kept, axis=1, keepdims=True))
    return jnp.concatenate(across, axis=1), jnp.concatenate(along, axis=0)


def remote(src, dst, send_sem, recv_sem, axis, index):
    return pltpu.make_async_remote_copy(
        src_ref=src,
        dst_ref=dst,
        send_sem=send_sem,
        recv_sem=recv_sem,
        device_id={axis: index},
        device_id_type=MESH,
    )


def signal_peers(barrier, axis, count):
    mine = lax.axis_index(axis)
    for d in range(1, count):
        pl.semaphore_signal(
            barrier,
            inc=1,
            device_id={axis: lax.rem(mine + d, count)},
            device_id_type=MESH,
        )


def sum_over_rows(count, packed, parts, total, scatter_send, scatter_recv, gather_send, gather_recv, between):
    mine = lax.axis_index("rows")
    share = PACKED // count

    def part(index):
        return pl.ds(pl.multiple_of(index * share, 8), share)

    scatter = []
    for d in range(1, count):
        peer = lax.rem(mine + d, count)
        copy = remote(packed.at[part(peer)], parts.at[d - 1], scatter_send.at[d - 1], scatter_recv.at[d - 1], "rows", peer)
        copy.start()
        scatter.append(copy)
    between()
    summed = packed[part(mine), :]
    for d in range(1, count):
        scatter[d - 1].wait_recv()
        summed = summed + parts[d - 1]
    total[part(mine), :] = summed
    gather = []
    for d in range(1, count):
        peer = lax.rem(mine + d, count)
        copy = remote(total.at[part(mine)], total.at[part(mine)], gather_send.at[d - 1], gather_recv.at[d - 1], "rows", peer)
        copy.start()
        gather.append(copy)
    for d in range(1, count):
        source = lax.rem(mine + count - d, count)
        remote(total.at[part(source)], total.at[part(source)], gather_send.at[d - 1], gather_recv.at[d - 1], "rows", source).wait_recv()
    for copy in scatter + gather:
        copy.wait_send()


def send_orders(pairs):
    if pairs != 8:
        return [[(me + d) % pairs for d in range(1, pairs)] for me in range(pairs)]
    orders = []
    for me in range(pairs):
        flips = [6, 7, 4, 5, 1, 2, 3] if 2 <= me < 6 else [2, 3, 1, 4, 5, 6, 7]
        orders.append([me ^ flip for flip in flips])
    return orders


def receive_orders(pairs):
    if pairs != 8:
        return [[(me + pairs - d) % pairs for d in range(1, pairs)] for me in range(pairs)]
    inner, outer = [2, 4, 5, 6, 7, 8, 9], [0, 1, 3, 10, 11, 12, 13]
    sends = send_orders(pairs)

    def due(source, me):
        return (inner if 2 <= source < 6 else outer)[sends[source].index(me)]

    return [
        sorted([source for source in range(pairs) if source != me], key=lambda source: due(source, me))
        for me in range(pairs)
    ]


def pick(orders, mine, step):
    chosen = jnp.int32(orders[0][step])
    for me in range(1, len(orders)):
        chosen = jnp.where(mine == me, jnp.int32(orders[me][step]), chosen)
    return chosen


def collect_kernel(
    pairs, rows, room,
    unit_ref, scale_ref, seating_ref, counts_ref, units_ref, gram_ref,
    unit, seated, landed, main, cross, packed, parts, total,
    send_sem, recv_sem, load_sem, out_sem, scatter_send, scatter_recv, gather_send, gather_recv,
):
    mine = lax.axis_index("pairs")
    to, from_ = send_orders(pairs), receive_orders(pairs)
    barrier = pltpu.get_barrier_semaphore()
    signal_peers(barrier, "pairs", pairs)
    signal_peers(barrier, "rows", rows)
    load = pltpu.make_async_copy(unit_ref.at[0, 0], unit, load_sem)
    load.start()
    main[...] = jnp.zeros_like(main)
    cross[...] = jnp.zeros_like(cross)
    band_row = lax.broadcasted_iota(jnp.int32, (BAND, BLOCK), 0)
    own_count = counts_ref[0, mine]
    load.wait()
    pl.semaphore_wait(barrier, pairs + rows - 2)

    blocks = unit.shape[1] // BLOCK

    def choose(ref, rows, seat):
        chosen = ref[rows, pl.ds(0, BLOCK)]
        at = jnp.broadcast_to(seat, chosen.shape)
        for index in range(1, blocks):
            chosen = jnp.where(at == index, ref[rows, pl.ds(index * BLOCK, BLOCK)], chosen)
        return chosen

    def fill(block, pair):
        for h in range(2):
            seat = seating_ref[2 * pair + h]
            scale = choose(scale_ref, pl.ds(0, 1), seat)

            def part(i, carry):
                rows = pl.ds(pl.multiple_of(i * BAND, BAND), BAND)
                live = band_row + i * BAND < own_count
                block[rows, pl.ds(h * BLOCK, BLOCK)] = jnp.where(live, choose(unit, rows, seat) * scale, 0.0)
                return carry

            lax.fori_loop(0, room // BAND, part, 0)

    def write_out(source):
        return pltpu.make_async_copy(landed.at[source], units_ref.at[source], out_sem.at[source])

    sends = []
    for step in range(pairs - 1):
        peer = pick(to, mine, step)
        fill(seated.at[step], peer)
        copy = remote(seated.at[step], landed.at[mine], send_sem.at[step], recv_sem.at[mine], "pairs", peer)
        copy.start()
        sends.append(copy)
    fill(landed.at[mine], mine)
    write_out(mine).start()
    add_gram(main, cross, landed[mine])
    sources = [pick(from_, mine, step) for step in range(pairs - 1)]
    for source in sources:
        remote(seated.at[0], landed.at[source], send_sem.at[0], recv_sem.at[source], "pairs", source).wait_recv()
        write_out(source).start()
        add_gram(main, cross, landed[source])
    pack_gram(main, cross, packed)
    sum_over_rows(rows, packed, parts, total, scatter_send, scatter_recv, gather_send, gather_recv, lambda: None)
    gram_ref[...] = total[...]
    for source in [mine, *sources]:
        write_out(source).wait()
    for copy in sends:
        copy.wait_send()


def gram_scratch(rows):
    return [
        pltpu.VMEM((WIDTH, WIDTH), jnp.float32),
        pltpu.VMEM((WIDTH, WIDTH), jnp.float32),
        pltpu.VMEM((PACKED, TILE), jnp.float32),
        pltpu.VMEM((rows - 1, PACKED // rows, TILE), jnp.float32),
        pltpu.VMEM((PACKED, TILE), jnp.float32),
    ]


def row_sems(rows):
    return [pltpu.SemaphoreType.DMA((rows - 1,))] * 4


ANY_SPEC = pl.BlockSpec(memory_space=pl.ANY)
VMEM_SPEC = pl.BlockSpec(memory_space=pltpu.VMEM)
SMEM_SPEC = pl.BlockSpec(memory_space=pltpu.SMEM)
PANEL_AND_GRAM = (
    jax.ShapeDtypeStruct((ROWS_DEV, WIDTH), jnp.float32),
    jax.ShapeDtypeStruct((PACKED, TILE), jnp.float32),
)


def collect(pairs, rows, unit_rows, channel_scale, seating, unit_counts):
    capacity, columns = unit_rows.shape[2:]
    units = (pairs, capacity, WIDTH)
    return pl.pallas_call(
        functools.partial(collect_kernel, pairs, rows, capacity),
        out_shape=(
            jax.ShapeDtypeStruct(units, jnp.float32),
            jax.ShapeDtypeStruct((PACKED, TILE), jnp.float32),
        ),
        in_specs=[ANY_SPEC, VMEM_SPEC, SMEM_SPEC, SMEM_SPEC],
        out_specs=(ANY_SPEC, VMEM_SPEC),
        scratch_shapes=[
            pltpu.VMEM((capacity, columns), jnp.float32),
            pltpu.VMEM((pairs - 1, capacity, WIDTH), jnp.float32),
            pltpu.VMEM(units, jnp.float32),
            *gram_scratch(rows),
            pltpu.SemaphoreType.DMA((pairs - 1,)),
            pltpu.SemaphoreType.DMA((pairs,)),
            pltpu.SemaphoreType.DMA,
            pltpu.SemaphoreType.DMA((pairs,)),
            *row_sems(rows),
        ],
        compiler_params=pltpu.CompilerParams(
            collective_id=0, has_side_effects=True, vmem_limit_bytes=VMEM_LIMIT
        ),
        name="collect",
    )(unit_rows, channel_scale, seating, unit_counts)


def exchange_kernel(
    pairs, rows,
    old_ref, panel_ref, gram_ref,
    landed, main, cross, packed, parts, total,
    up_send, up_recv, down_send, down_recv, scatter_send, scatter_recv, gather_send, gather_recv,
):
    mine = lax.axis_index("pairs")
    last = pairs - 1
    barrier = pltpu.get_barrier_semaphore()
    signal_peers(barrier, "rows", rows)

    def greet(index):
        pl.semaphore_signal(barrier, inc=1, device_id={"pairs": index}, device_id_type=MESH)

    @pl.when(mine < last)
    def _():
        greet(mine + 1)

    @pl.when(mine > 0)
    def _():
        greet(mine - 1)

    main[...] = jnp.zeros_like(main)
    cross[...] = jnp.zeros_like(cross)
    greeted = jnp.where(mine < last, 1, 0) + jnp.where(mine > 0, 1, 0)
    pl.semaphore_wait(barrier, rows - 1 + greeted)

    size = ROWS_DEV // CHUNKS
    upper, lower = pl.ds(0, BLOCK), pl.ds(BLOCK, BLOCK)

    def up(c, source):
        here = pl.ds(c * size, size)
        return remote(old_ref.at[here, source], landed.at[here, upper], up_send.at[c], up_recv.at[c], "pairs", mine + 1)

    def down(c):
        here = pl.ds(c * size, size)
        return remote(old_ref.at[here, lower], landed.at[here, lower], down_send.at[c], down_recv.at[c], "pairs", mine - 1)

    for c in range(CHUNKS):
        @pl.when(mine == 0)
        def _():
            up(c, lower).start()

        @pl.when((mine > 0) & (mine < last))
        def _():
            up(c, upper).start()

        @pl.when(mine > 0)
        def _():
            down(c).start()

    @pl.when(mine == 0)
    def _():
        landed[:, upper] = old_ref[:, upper]

    @pl.when(mine == last)
    def _():
        landed[:, lower] = old_ref[:, upper]

    for c in range(CHUNKS):
        @pl.when(mine > 0)
        def _():
            up(c, upper).wait_recv()

        @pl.when(mine < last)
        def _():
            down(c).wait_recv()

        add_gram(main, cross, landed[pl.ds(c * size, size), :])
    pack_gram(main, cross, packed)

    def hand_over():
        panel_ref[...] = landed[...]

    sum_over_rows(rows, packed, parts, total, scatter_send, scatter_recv, gather_send, gather_recv, hand_over)
    gram_ref[...] = total[...]
    for c in range(CHUNKS):
        @pl.when(mine < last)
        def _():
            up(c, upper).wait_send()

        @pl.when(mine > 0)
        def _():
            down(c).wait_send()


def exchange(pairs, rows, panel):
    return pl.pallas_call(
        functools.partial(exchange_kernel, pairs, rows),
        out_shape=PANEL_AND_GRAM,
        in_specs=[VMEM_SPEC],
        out_specs=(VMEM_SPEC, VMEM_SPEC),
        scratch_shapes=[
            pltpu.VMEM((ROWS_DEV, WIDTH), jnp.float32),
            *gram_scratch(rows),
            *[pltpu.SemaphoreType.DMA((CHUNKS,))] * 4,
            *row_sems(rows),
        ],
        compiler_params=pltpu.CompilerParams(
            collective_id=1, has_side_effects=True, vmem_limit_bytes=VMEM_LIMIT
        ),
        name="exchange",
    )(panel)


def turn_units_kernel(counts_ref, packed, units_ref, out, units, panel, load_sem, *scratch):
    pairs, room = units.shape[:2]
    load = pltpu.make_async_copy(units_ref, units, load_sem)
    load.start()

    def compact():
        load.wait()
        start = jnp.int32(0)
        groups = room // ALIGN
        lane_row = lax.broadcasted_iota(jnp.int32, (groups + 1, ALIGN, WIDTH), 1)
        for k in range(pairs):
            first = pl.multiple_of(start & -ALIGN, ALIGN)
            shift = start & (ALIGN - 1)
            turned = pltpu.roll(units[k].reshape(groups, ALIGN, WIDTH), shift, 1)
            before = panel[pl.ds(first, ALIGN), :].reshape(1, ALIGN, WIDTH)
            shifted = jnp.where(
                lane_row < shift,
                jnp.concatenate([before, turned], axis=0),
                jnp.concatenate([turned, turned[-1:]], axis=0),
            )
            panel[pl.ds(first, room + ALIGN), :] = shifted.reshape(room + ALIGN, WIDTH)
            start = start + counts_ref[0, k]

    turn_panel(packed, panel, out, compact, *scratch)


def turn_kernel(packed, panel, out, *scratch):
    turn_panel(packed, panel, out, lambda: None, *scratch)


def turn_panel(packed, panel, out, prepare, gram, tangent, square, change):
    diag_row, diag_col = unpack_gram(packed, gram)
    tangent[...] = 0.5 * (
        gram[...] * (diag_row - diag_col) / (2.0 * (diag_col**2 + diag_row**2) + epsilon)
    )
    t_halves = halves(tangent[...])
    square[...] = dot_halves(t_halves, t_halves)
    m_high = square[...].astype(jnp.bfloat16)
    fourth = dot_once(m_high, m_high)
    rest = jnp.sum(fourth * fourth)
    short = rest <= SERIES_BOUND

    @pl.when(short)
    def _():
        first = tangent[...] + square[...]
        second = first + dot_once(first, m_high)
        change[...] = 2.0 * (second + dot_once(second, fourth))

    @pl.when(jnp.logical_not(short))
    def _():
        exact = functools.partial(
            jnp.dot, precision=lax.Precision.HIGHEST, preferred_element_type=jnp.float32
        )
        eye = (
            lax.broadcasted_iota(jnp.int32, (WIDTH, WIDTH), 0)
            == lax.broadcasted_iota(jnp.int32, (WIDTH, WIDTH), 1)
        )
        square[...] = exact(tangent[...], tangent[...])
        bound = jnp.sqrt(jnp.sqrt(jnp.full((1, 1), rest, jnp.float32))) * 1.01
        change[...] = jnp.where(eye, 2.0 / (2.0 + bound), 0.0)

        def newton(step, carry):
            inverse = change[...]
            residual = jnp.where(eye, 1.0, 0.0) - inverse + exact(square[...], inverse)
            change[...] = inverse + exact(inverse, residual)
            return carry

        lax.fori_loop(0, NEWTON_STEPS, newton, 0)
        change[...] = 2.0 * exact(tangent[...] + square[...], change[...])

    prepare()
    d_halves = halves(change[...])
    size = ROWS_DEV // CHUNKS

    def apply(c, carry):
        here = pl.ds(pl.multiple_of(c * size, size), size)
        block = panel[here, :]
        out[here, :] = block + dot_halves(halves(block), d_halves)
        return carry

    lax.fori_loop(0, CHUNKS, apply, 0)


def turn_units(unit_counts, packed, units):
    pairs, room = units.shape[:2]
    return pl.pallas_call(
        turn_units_kernel,
        out_shape=PANEL_AND_GRAM[0],
        in_specs=[SMEM_SPEC, VMEM_SPEC, ANY_SPEC],
        out_specs=VMEM_SPEC,
        scratch_shapes=[
            pltpu.VMEM(units.shape, jnp.float32),
            pltpu.VMEM((ROWS_DEV + room + ALIGN, WIDTH), jnp.float32),
            pltpu.SemaphoreType.DMA,
            *[pltpu.VMEM((WIDTH, WIDTH), jnp.float32)] * 4,
        ],
        compiler_params=pltpu.CompilerParams(vmem_limit_bytes=VMEM_LIMIT),
        name="turn_units",
    )(unit_counts, packed, units)


def turn(packed, panel):
    return pl.pallas_call(
        turn_kernel,
        out_shape=PANEL_AND_GRAM[0],
        in_specs=[VMEM_SPEC, VMEM_SPEC],
        out_specs=VMEM_SPEC,
        scratch_shapes=[pltpu.VMEM((WIDTH, WIDTH), jnp.float32)] * 4,
        compiler_params=pltpu.CompilerParams(vmem_limit_bytes=VMEM_LIMIT),
        name="turn",
    )(packed, panel)


def local(pairs, rows, unit_rows, unit_counts, seating, channel_scale):
    units, gram = collect(pairs, rows, unit_rows, channel_scale[None, :], seating, unit_counts)
    panel = turn_units(unit_counts, gram, units)
    for round_index in range(1, ROUNDS):
        panel, gram = exchange(pairs, rows, panel)
        panel = turn(gram, panel)
    return panel


def solution(mesh):
    return jax.shard_map(
        functools.partial(local, mesh.shape["pairs"], mesh.shape["rows"]),
        mesh=mesh,
        in_specs=(P("rows", "pairs", None, None), P("rows", None), P(), P()),
        out_specs=P("rows", "pairs"),
        check_vma=False,
    )
```

```python
import functools

import jax
import jax.numpy as jnp
from jax import lax
from jax.experimental import pallas as pl
from jax.experimental.pallas import tpu as pltpu
from jax.sharding import PartitionSpec as P

ROWS_DEV = 1024
BLOCK = 256
ROUNDS = 2
WIDTH = 2 * BLOCK
TILE = 128
ALIGN = 8
BAND = 64
CHUNKS = 4
NEWTON_STEPS = 18
SERIES_BOUND = 1e-6
VMEM_LIMIT = 48 * 1024 * 1024

epsilon = 1e-06

MESH = pl.DeviceIdType.MESH
TILES = WIDTH // TILE
OFF_DIAGONAL = [(i, j) for i in range(TILES) for j in range(i + 1, TILES)]
DIAGONAL_AT = len(OFF_DIAGONAL) * TILE
EXTRA_AT = DIAGONAL_AT + TILES // 2 * TILE
EXTRA = 64
PACKED = EXTRA_AT + EXTRA


def halves(x):
    high = x.astype(jnp.bfloat16)
    low = (x - high.astype(jnp.float32)).astype(jnp.bfloat16)
    return high, low


def dot_halves(a, b):
    mul = functools.partial(jnp.dot, preferred_element_type=jnp.float32)
    return mul(a[0], b[0]) + (mul(a[0], b[1]) + mul(a[1], b[0]))


def dot_once(a, b):
    return jnp.dot(a.astype(jnp.bfloat16), b.astype(jnp.bfloat16), preferred_element_type=jnp.float32)


def add_gram(main, cross, block):
    high, low = halves(block)
    mul = functools.partial(
        lax.dot_general,
        dimension_numbers=(((0,), (0,)), ((), ())),
        preferred_element_type=jnp.float32,
    )
    main[...] += mul(high, high)
    cross[...] += mul(high, low)


def tile_iotas():
    shape = (TILE, TILE)
    return lax.broadcasted_iota(jnp.int32, shape, 0), lax.broadcasted_iota(jnp.int32, shape, 1)


def pack_gram(main, cross, packed):
    def tile(i, j):
        rows, cols = pl.ds(i * TILE, TILE), pl.ds(j * TILE, TILE)
        return main[rows, cols] + cross[rows, cols] + cross[cols, rows].T

    row, col = tile_iotas()
    for t, (i, j) in enumerate(OFF_DIAGONAL):
        packed[pl.ds(t * TILE, TILE), :] = tile(i, j)
    packed[pl.ds(EXTRA_AT, EXTRA), :] = jnp.zeros((EXTRA, TILE), jnp.float32)
    for t in range(TILES // 2):
        lower = tile(2 * t + 1, 2 * t + 1)
        packed[pl.ds(DIAGONAL_AT + t * TILE, TILE), :] = jnp.where(row <= col, tile(2 * t, 2 * t), lower)
        packed[pl.ds(EXTRA_AT + t, 1), :] = jnp.sum(jnp.where(row == col, lower, 0.0), axis=0, keepdims=True)


def unpack_gram(packed, gram):
    row, col = tile_iotas()
    across, along = [], []
    for t, (i, j) in enumerate(OFF_DIAGONAL):
        tile = packed[pl.ds(t * TILE, TILE), :]
        gram[pl.ds(i * TILE, TILE), pl.ds(j * TILE, TILE)] = tile
        gram[pl.ds(j * TILE, TILE), pl.ds(i * TILE, TILE)] = tile.T
    for t in range(TILES // 2):
        both = packed[pl.ds(DIAGONAL_AT + t * TILE, TILE), :]
        flipped = both.T
        upper = jnp.where(row <= col, both, flipped)
        lower = jnp.where(row > col, both, flipped)
        lower = jnp.where(row == col, packed[pl.ds(EXTRA_AT + t, 1), :], lower)
        for i, tile in ((2 * t, upper), (2 * t + 1, lower)):
            gram[pl.ds(i * TILE, TILE), pl.ds(i * TILE, TILE)] = tile
            kept = jnp.where(row == col, tile, 0.0)
            across.append(jnp.sum(kept, axis=0, keepdims=True))
            along.append(jnp.sum(kept, axis=1, keepdims=True))
    return jnp.concatenate(across, axis=1), jnp.concatenate(along, axis=0)


def remote(src, dst, send_sem, recv_sem, axis, index):
    return pltpu.make_async_remote_copy(
        src_ref=src,
        dst_ref=dst,
        send_sem=send_sem,
        recv_sem=recv_sem,
        device_id={axis: index},
        device_id_type=MESH,
    )


def signal_peers(barrier, axis, count):
    mine = lax.axis_index(axis)
    for d in range(1, count):
        pl.semaphore_signal(
            barrier,
            inc=1,
            device_id={axis: lax.rem(mine + d, count)},
            device_id_type=MESH,
        )


def sum_over_rows(count, packed, parts, total, scatter_send, scatter_recv, gather_send, gather_recv, between):
    mine = lax.axis_index("rows")
    share = PACKED // count

    def part(index):
        return pl.ds(pl.multiple_of(index * share, 8), share)

    scatter = []
    for d in range(1, count):
        peer = lax.rem(mine + d, count)
        copy = remote(packed.at[part(peer)], parts.at[d - 1], scatter_send.at[d - 1], scatter_recv.at[d - 1], "rows", peer)
        copy.start()
        scatter.append(copy)
    between()
    summed = packed[part(mine), :]
    for d in range(1, count):
        scatter[d - 1].wait_recv()
        summed = summed + parts[d - 1]
    total[part(mine), :] = summed
    gather = []
    for d in range(1, count):
        peer = lax.rem(mine + d, count)
        copy = remote(total.at[part(mine)], total.at[part(mine)], gather_send.at[d - 1], gather_recv.at[d - 1], "rows", peer)
        copy.start()
        gather.append(copy)
    for d in range(1, count):
        source = lax.rem(mine + count - d, count)
        remote(total.at[part(source)], total.at[part(source)], gather_send.at[d - 1], gather_recv.at[d - 1], "rows", source).wait_recv()
    for copy in scatter + gather:
        copy.wait_send()


def collect_kernel(
    pairs, rows, room,
    unit_ref, scale_ref, seating_ref, counts_ref, units_ref, gram_ref,
    unit, seated, landed, main, cross, packed, parts, total,
    send_sem, recv_sem, load_sem, out_sem, scatter_send, scatter_recv, gather_send, gather_recv,
):
    mine = lax.axis_index("pairs")
    barrier = pltpu.get_barrier_semaphore()
    signal_peers(barrier, "pairs", pairs)
    signal_peers(barrier, "rows", rows)
    load = pltpu.make_async_copy(unit_ref.at[0, 0], unit, load_sem)
    load.start()
    main[...] = jnp.zeros_like(main)
    cross[...] = jnp.zeros_like(cross)
    band_row = lax.broadcasted_iota(jnp.int32, (BAND, BLOCK), 0)
    own_count = counts_ref[0, mine]
    load.wait()
    pl.semaphore_wait(barrier, pairs + rows - 2)

    blocks = unit.shape[1] // BLOCK

    def choose(ref, rows, seat):
        chosen = ref[rows, pl.ds(0, BLOCK)]
        at = jnp.broadcast_to(seat, chosen.shape)
        for index in range(1, blocks):
            chosen = jnp.where(at == index, ref[rows, pl.ds(index * BLOCK, BLOCK)], chosen)
        return chosen

    def fill(block, pair):
        for h in range(2):
            seat = seating_ref[2 * pair + h]
            scale = choose(scale_ref, pl.ds(0, 1), seat)

            def part(i, carry):
                rows = pl.ds(pl.multiple_of(i * BAND, BAND), BAND)
                live = band_row + i * BAND < own_count
                block[rows, pl.ds(h * BLOCK, BLOCK)] = jnp.where(live, choose(unit, rows, seat) * scale, 0.0)
                return carry

            lax.fori_loop(0, room // BAND, part, 0)

    def write_out(source):
        return pltpu.make_async_copy(landed.at[source], units_ref.at[source], out_sem.at[source])

    sends = []
    for step in range(pairs - 1):
        peer = lax.rem(mine + step + 1, pairs)
        fill(seated.at[step], peer)
        copy = remote(seated.at[step], landed.at[mine], send_sem.at[step], recv_sem.at[mine], "pairs", peer)
        copy.start()
        sends.append(copy)
    fill(landed.at[mine], mine)
    write_out(mine).start()
    add_gram(main, cross, landed[mine])
    sources = [lax.rem(mine + pairs - d, pairs) for d in range(1, pairs)]
    for source in sources:
        remote(seated.at[0], landed.at[source], send_sem.at[0], recv_sem.at[source], "pairs", source).wait_recv()
        write_out(source).start()
        add_gram(main, cross, landed[source])
    pack_gram(main, cross, packed)
    sum_over_rows(rows, packed, parts, total, scatter_send, scatter_recv, gather_send, gather_recv, lambda: None)
    gram_ref[...] = total[...]
    for source in [mine, *sources]:
        write_out(source).wait()
    for copy in sends:
        copy.wait_send()


def gram_scratch(rows):
    return [
        pltpu.VMEM((WIDTH, WIDTH), jnp.float32),
        pltpu.VMEM((WIDTH, WIDTH), jnp.float32),
        pltpu.VMEM((PACKED, TILE), jnp.float32),
        pltpu.VMEM((rows - 1, PACKED // rows, TILE), jnp.float32),
        pltpu.VMEM((PACKED, TILE), jnp.float32),
    ]


def row_sems(rows):
    return [pltpu.SemaphoreType.DMA((rows - 1,))] * 4


ANY_SPEC = pl.BlockSpec(memory_space=pl.ANY)
VMEM_SPEC = pl.BlockSpec(memory_space=pltpu.VMEM)
SMEM_SPEC = pl.BlockSpec(memory_space=pltpu.SMEM)
PANEL_AND_GRAM = (
    jax.ShapeDtypeStruct((ROWS_DEV, WIDTH), jnp.float32),
    jax.ShapeDtypeStruct((PACKED, TILE), jnp.float32),
)


def collect(pairs, rows, unit_rows, channel_scale, seating, unit_counts):
    capacity, columns = unit_rows.shape[2:]
    units = (pairs, capacity, WIDTH)
    return pl.pallas_call(
        functools.partial(collect_kernel, pairs, rows, capacity),
        out_shape=(
            jax.ShapeDtypeStruct(units, jnp.float32),
            jax.ShapeDtypeStruct((PACKED, TILE), jnp.float32),
        ),
        in_specs=[ANY_SPEC, VMEM_SPEC, SMEM_SPEC, SMEM_SPEC],
        out_specs=(ANY_SPEC, VMEM_SPEC),
        scratch_shapes=[
            pltpu.VMEM((capacity, columns), jnp.float32),
            pltpu.VMEM((pairs - 1, capacity, WIDTH), jnp.float32),
            pltpu.VMEM(units, jnp.float32),
            *gram_scratch(rows),
            pltpu.SemaphoreType.DMA((pairs - 1,)),
            pltpu.SemaphoreType.DMA((pairs,)),
            pltpu.SemaphoreType.DMA,
            pltpu.SemaphoreType.DMA((pairs,)),
            *row_sems(rows),
        ],
        compiler_params=pltpu.CompilerParams(
            collective_id=0, has_side_effects=True, vmem_limit_bytes=VMEM_LIMIT
        ),
        name="collect",
    )(unit_rows, channel_scale, seating, unit_counts)


def exchange_kernel(
    pairs, rows,
    old_ref, panel_ref, gram_ref,
    landed, main, cross, packed, parts, total,
    up_send, up_recv, down_send, down_recv, scatter_send, scatter_recv, gather_send, gather_recv,
):
    mine = lax.axis_index("pairs")
    last = pairs - 1
    barrier = pltpu.get_barrier_semaphore()
    signal_peers(barrier, "rows", rows)

    def greet(index):
        pl.semaphore_signal(barrier, inc=1, device_id={"pairs": index}, device_id_type=MESH)

    @pl.when(mine < last)
    def _():
        greet(mine + 1)

    @pl.when(mine > 0)
    def _():
        greet(mine - 1)

    main[...] = jnp.zeros_like(main)
    cross[...] = jnp.zeros_like(cross)
    greeted = jnp.where(mine < last, 1, 0) + jnp.where(mine > 0, 1, 0)
    pl.semaphore_wait(barrier, rows - 1 + greeted)

    size = ROWS_DEV // CHUNKS
    upper, lower = pl.ds(0, BLOCK), pl.ds(BLOCK, BLOCK)

    def up(c, source):
        here = pl.ds(c * size, size)
        return remote(old_ref.at[here, source], landed.at[here, upper], up_send.at[c], up_recv.at[c], "pairs", mine + 1)

    def down(c):
        here = pl.ds(c * size, size)
        return remote(old_ref.at[here, lower], landed.at[here, lower], down_send.at[c], down_recv.at[c], "pairs", mine - 1)

    for c in range(CHUNKS):
        @pl.when(mine == 0)
        def _():
            up(c, lower).start()

        @pl.when((mine > 0) & (mine < last))
        def _():
            up(c, upper).start()

        @pl.when(mine > 0)
        def _():
            down(c).start()

    @pl.when(mine == 0)
    def _():
        landed[:, upper] = old_ref[:, upper]

    @pl.when(mine == last)
    def _():
        landed[:, lower] = old_ref[:, upper]

    for c in range(CHUNKS):
        @pl.when(mine > 0)
        def _():
            up(c, upper).wait_recv()

        @pl.when(mine < last)
        def _():
            down(c).wait_recv()

        add_gram(main, cross, landed[pl.ds(c * size, size), :])
    pack_gram(main, cross, packed)

    def hand_over():
        panel_ref[...] = landed[...]

    sum_over_rows(rows, packed, parts, total, scatter_send, scatter_recv, gather_send, gather_recv, hand_over)
    gram_ref[...] = total[...]
    for c in range(CHUNKS):
        @pl.when(mine < last)
        def _():
            up(c, upper).wait_send()

        @pl.when(mine > 0)
        def _():
            down(c).wait_send()


def exchange(pairs, rows, panel):
    return pl.pallas_call(
        functools.partial(exchange_kernel, pairs, rows),
        out_shape=PANEL_AND_GRAM,
        in_specs=[VMEM_SPEC],
        out_specs=(VMEM_SPEC, VMEM_SPEC),
        scratch_shapes=[
            pltpu.VMEM((ROWS_DEV, WIDTH), jnp.float32),
            *gram_scratch(rows),
            *[pltpu.SemaphoreType.DMA((CHUNKS,))] * 4,
            *row_sems(rows),
        ],
        compiler_params=pltpu.CompilerParams(
            collective_id=1, has_side_effects=True, vmem_limit_bytes=VMEM_LIMIT
        ),
        name="exchange",
    )(panel)


def turn_units_kernel(counts_ref, packed, units_ref, out, units, panel, load_sem, *scratch):
    pairs, room = units.shape[:2]
    load = pltpu.make_async_copy(units_ref, units, load_sem)
    load.start()

    def compact():
        load.wait()
        start = jnp.int32(0)
        groups = room // ALIGN
        lane_row = lax.broadcasted_iota(jnp.int32, (groups + 1, ALIGN, WIDTH), 1)
        for k in range(pairs):
            first = pl.multiple_of(start & -ALIGN, ALIGN)
            shift = start & (ALIGN - 1)
            turned = pltpu.roll(units[k].reshape(groups, ALIGN, WIDTH), shift, 1)
            before = panel[pl.ds(first, ALIGN), :].reshape(1, ALIGN, WIDTH)
            shifted = jnp.where(
                lane_row < shift,
                jnp.concatenate([before, turned], axis=0),
                jnp.concatenate([turned, turned[-1:]], axis=0),
            )
            panel[pl.ds(first, room + ALIGN), :] = shifted.reshape(room + ALIGN, WIDTH)
            start = start + counts_ref[0, k]

    turn_panel(packed, panel, out, compact, *scratch)


def turn_kernel(packed, panel, out, *scratch):
    turn_panel(packed, panel, out, lambda: None, *scratch)


def turn_panel(packed, panel, out, prepare, gram, tangent, square, change):
    diag_row, diag_col = unpack_gram(packed, gram)
    tangent[...] = 0.5 * (
        gram[...] * (diag_row - diag_col) / (2.0 * (diag_col**2 + diag_row**2) + epsilon)
    )
    t_halves = halves(tangent[...])
    square[...] = dot_halves(t_halves, t_halves)
    m_high = square[...].astype(jnp.bfloat16)
    fourth = dot_once(m_high, m_high)
    rest = jnp.sum(fourth * fourth)
    short = rest <= SERIES_BOUND

    @pl.when(short)
    def _():
        first = tangent[...] + square[...]
        second = first + dot_once(first, m_high)
        change[...] = 2.0 * (second + dot_once(second, fourth))

    @pl.when(jnp.logical_not(short))
    def _():
        exact = functools.partial(
            jnp.dot, precision=lax.Precision.HIGHEST, preferred_element_type=jnp.float32
        )
        eye = (
            lax.broadcasted_iota(jnp.int32, (WIDTH, WIDTH), 0)
            == lax.broadcasted_iota(jnp.int32, (WIDTH, WIDTH), 1)
        )
        square[...] = exact(tangent[...], tangent[...])
        bound = jnp.sqrt(jnp.sqrt(jnp.full((1, 1), rest, jnp.float32))) * 1.01
        change[...] = jnp.where(eye, 2.0 / (2.0 + bound), 0.0)

        def newton(step, carry):
            inverse = change[...]
            residual = jnp.where(eye, 1.0, 0.0) - inverse + exact(square[...], inverse)
            change[...] = inverse + exact(inverse, residual)
            return carry

        lax.fori_loop(0, NEWTON_STEPS, newton, 0)
        change[...] = 2.0 * exact(tangent[...] + square[...], change[...])

    prepare()
    d_halves = halves(change[...])
    size = ROWS_DEV // CHUNKS

    def apply(c, carry):
        here = pl.ds(pl.multiple_of(c * size, size), size)
        block = panel[here, :]
        out[here, :] = block + dot_halves(halves(block), d_halves)
        return carry

    lax.fori_loop(0, CHUNKS, apply, 0)


def turn_units(unit_counts, packed, units):
    pairs, room = units.shape[:2]
    return pl.pallas_call(
        turn_units_kernel,
        out_shape=PANEL_AND_GRAM[0],
        in_specs=[SMEM_SPEC, VMEM_SPEC, ANY_SPEC],
        out_specs=VMEM_SPEC,
        scratch_shapes=[
            pltpu.VMEM(units.shape, jnp.float32),
            pltpu.VMEM((ROWS_DEV + room + ALIGN, WIDTH), jnp.float32),
            pltpu.SemaphoreType.DMA,
            *[pltpu.VMEM((WIDTH, WIDTH), jnp.float32)] * 4,
        ],
        compiler_params=pltpu.CompilerParams(vmem_limit_bytes=VMEM_LIMIT),
        name="turn_units",
    )(unit_counts, packed, units)


def turn(packed, panel):
    return pl.pallas_call(
        turn_kernel,
        out_shape=PANEL_AND_GRAM[0],
        in_specs=[VMEM_SPEC, VMEM_SPEC],
        out_specs=VMEM_SPEC,
        scratch_shapes=[pltpu.VMEM((WIDTH, WIDTH), jnp.float32)] * 4,
        compiler_params=pltpu.CompilerParams(vmem_limit_bytes=VMEM_LIMIT),
        name="turn",
    )(packed, panel)


def local(pairs, rows, unit_rows, unit_counts, seating, channel_scale):
    units, gram = collect(pairs, rows, unit_rows, channel_scale[None, :], seating, unit_counts)
    panel = turn_units(unit_counts, gram, units)
    for round_index in range(1, ROUNDS):
        panel, gram = exchange(pairs, rows, panel)
        panel = turn(gram, panel)
    return panel


def solution(mesh):
    return jax.shard_map(
        functools.partial(local, mesh.shape["pairs"], mesh.shape["rows"]),
        mesh=mesh,
        in_specs=(P("rows", "pairs", None, None), P("rows", None), P(), P()),
        out_specs=P("rows", "pairs"),
        check_vma=False,
    )
```

```python
import functools

import jax
import jax.numpy as jnp
from jax import lax
from jax.experimental import pallas as pl
from jax.experimental.pallas import tpu as pltpu
from jax.sharding import PartitionSpec as P

ROWS_DEV = 1024
BLOCK = 256
ROUNDS = 2
WIDTH = 2 * BLOCK
TILE = 128
ALIGN = 8
BAND = 64
CHUNKS = 4
NEWTON_STEPS = 18
SERIES_BOUND = 1e-6
VMEM_LIMIT = 48 * 1024 * 1024

epsilon = 1e-06

MESH = pl.DeviceIdType.MESH
TILES = WIDTH // TILE
OFF_DIAGONAL = [(i, j) for i in range(TILES) for j in range(i + 1, TILES)]
DIAGONAL_AT = len(OFF_DIAGONAL) * TILE
EXTRA_AT = DIAGONAL_AT + TILES // 2 * TILE
EXTRA = 64
PACKED = EXTRA_AT + EXTRA


def halves(x):
    high = x.astype(jnp.bfloat16)
    low = (x - high.astype(jnp.float32)).astype(jnp.bfloat16)
    return high, low


def dot_halves(a, b):
    mul = functools.partial(jnp.dot, preferred_element_type=jnp.float32)
    return mul(a[0], b[0]) + (mul(a[0], b[1]) + mul(a[1], b[0]))


def dot_once(a, b):
    return jnp.dot(a.astype(jnp.bfloat16), b.astype(jnp.bfloat16), preferred_element_type=jnp.float32)


def add_gram(main, cross, block):
    high, low = halves(block)
    mul = functools.partial(
        lax.dot_general,
        dimension_numbers=(((0,), (0,)), ((), ())),
        preferred_element_type=jnp.float32,
    )
    main[...] += mul(high, high)
    cross[...] += mul(high, low)


def tile_iotas():
    shape = (TILE, TILE)
    return lax.broadcasted_iota(jnp.int32, shape, 0), lax.broadcasted_iota(jnp.int32, shape, 1)


def pack_gram(main, cross, packed):
    def tile(i, j):
        rows, cols = pl.ds(i * TILE, TILE), pl.ds(j * TILE, TILE)
        return main[rows, cols] + cross[rows, cols] + cross[cols, rows].T

    row, col = tile_iotas()
    for t, (i, j) in enumerate(OFF_DIAGONAL):
        packed[pl.ds(t * TILE, TILE), :] = tile(i, j)
    packed[pl.ds(EXTRA_AT, EXTRA), :] = jnp.zeros((EXTRA, TILE), jnp.float32)
    for t in range(TILES // 2):
        lower = tile(2 * t + 1, 2 * t + 1)
        packed[pl.ds(DIAGONAL_AT + t * TILE, TILE), :] = jnp.where(row <= col, tile(2 * t, 2 * t), lower)
        packed[pl.ds(EXTRA_AT + t, 1), :] = jnp.sum(jnp.where(row == col, lower, 0.0), axis=0, keepdims=True)


def unpack_gram(packed, gram):
    row, col = tile_iotas()
    across, along = [], []
    for t, (i, j) in enumerate(OFF_DIAGONAL):
        tile = packed[pl.ds(t * TILE, TILE), :]
        gram[pl.ds(i * TILE, TILE), pl.ds(j * TILE, TILE)] = tile
        gram[pl.ds(j * TILE, TILE), pl.ds(i * TILE, TILE)] = tile.T
    for t in range(TILES // 2):
        both = packed[pl.ds(DIAGONAL_AT + t * TILE, TILE), :]
        flipped = both.T
        upper = jnp.where(row <= col, both, flipped)
        lower = jnp.where(row > col, both, flipped)
        lower = jnp.where(row == col, packed[pl.ds(EXTRA_AT + t, 1), :], lower)
        for i, tile in ((2 * t, upper), (2 * t + 1, lower)):
            gram[pl.ds(i * TILE, TILE), pl.ds(i * TILE, TILE)] = tile
            kept = jnp.where(row == col, tile, 0.0)
            across.append(jnp.sum(kept, axis=0, keepdims=True))
            along.append(jnp.sum(kept, axis=1, keepdims=True))
    return jnp.concatenate(across, axis=1), jnp.concatenate(along, axis=0)


def remote(src, dst, send_sem, recv_sem, axis, index):
    return pltpu.make_async_remote_copy(
        src_ref=src,
        dst_ref=dst,
        send_sem=send_sem,
        recv_sem=recv_sem,
        device_id={axis: index},
        device_id_type=MESH,
    )


def signal_peers(barrier, axis, count):
    mine = lax.axis_index(axis)
    for d in range(1, count):
        pl.semaphore_signal(
            barrier,
            inc=1,
            device_id={axis: lax.rem(mine + d, count)},
            device_id_type=MESH,
        )


def sum_over_rows(count, packed, parts, total, scatter_send, scatter_recv, gather_send, gather_recv, between):
    mine = lax.axis_index("rows")
    share = PACKED // count

    def part(index):
        return pl.ds(pl.multiple_of(index * share, 8), share)

    scatter = []
    for d in range(1, count):
        peer = lax.rem(mine + d, count)
        copy = remote(packed.at[part(peer)], parts.at[d - 1], scatter_send.at[d - 1], scatter_recv.at[d - 1], "rows", peer)
        copy.start()
        scatter.append(copy)
    between()
    summed = packed[part(mine), :]
    for d in range(1, count):
        scatter[d - 1].wait_recv()
        summed = summed + parts[d - 1]
    total[part(mine), :] = summed
    gather = []
    for d in range(1, count):
        peer = lax.rem(mine + d, count)
        copy = remote(total.at[part(mine)], total.at[part(mine)], gather_send.at[d - 1], gather_recv.at[d - 1], "rows", peer)
        copy.start()
        gather.append(copy)
    for d in range(1, count):
        source = lax.rem(mine + count - d, count)
        remote(total.at[part(source)], total.at[part(source)], gather_send.at[d - 1], gather_recv.at[d - 1], "rows", source).wait_recv()
    for copy in scatter + gather:
        copy.wait_send()


def collect_kernel(
    pairs, rows, room,
    unit_ref, scale_ref, seating_ref, counts_ref, units_ref, gram_ref,
    unit, seated, landed, main, cross, packed, parts, total,
    send_sem, recv_sem, load_sem, out_sem, scatter_send, scatter_recv, gather_send, gather_recv,
):
    mine = lax.axis_index("pairs")
    barrier = pltpu.get_barrier_semaphore()
    signal_peers(barrier, "pairs", pairs)
    signal_peers(barrier, "rows", rows)
    load = pltpu.make_async_copy(unit_ref.at[0, 0], unit, load_sem)
    load.start()
    main[...] = jnp.zeros_like(main)
    cross[...] = jnp.zeros_like(cross)
    band_row = lax.broadcasted_iota(jnp.int32, (BAND, BLOCK), 0)
    own_count = counts_ref[0, mine]
    load.wait()
    pl.semaphore_wait(barrier, pairs + rows - 2)

    blocks = unit.shape[1] // BLOCK

    def choose(ref, rows, seat):
        chosen = ref[rows, pl.ds(0, BLOCK)]
        at = jnp.broadcast_to(seat, chosen.shape)
        for index in range(1, blocks):
            chosen = jnp.where(at == index, ref[rows, pl.ds(index * BLOCK, BLOCK)], chosen)
        return chosen

    def fill(block, pair):
        for h in range(2):
            seat = seating_ref[2 * pair + h]
            scale = choose(scale_ref, pl.ds(0, 1), seat)

            def part(i, carry):
                rows = pl.ds(pl.multiple_of(i * BAND, BAND), BAND)
                live = band_row + i * BAND < own_count
                block[rows, pl.ds(h * BLOCK, BLOCK)] = jnp.where(live, choose(unit, rows, seat) * scale, 0.0)
                return carry

            lax.fori_loop(0, room // BAND, part, 0)

    def write_out(source):
        return pltpu.make_async_copy(landed.at[source], units_ref.at[source], out_sem.at[source])

    sends = []
    farthest_first = sorted(range(1, pairs), key=lambda d: abs(d - pairs // 2))
    for step, d in enumerate(farthest_first):
        peer = lax.rem(mine + d, pairs)
        fill(seated.at[step], peer)
        copy = remote(seated.at[step], landed.at[mine], send_sem.at[step], recv_sem.at[mine], "pairs", peer)
        copy.start()
        sends.append(copy)
    fill(landed.at[mine], mine)
    write_out(mine).start()
    add_gram(main, cross, landed[mine])
    sources = [lax.rem(mine + pairs - d, pairs) for d in farthest_first]
    for source in sources:
        remote(seated.at[0], landed.at[source], send_sem.at[0], recv_sem.at[source], "pairs", source).wait_recv()
        write_out(source).start()
        add_gram(main, cross, landed[source])
    pack_gram(main, cross, packed)
    sum_over_rows(rows, packed, parts, total, scatter_send, scatter_recv, gather_send, gather_recv, lambda: None)
    gram_ref[...] = total[...]
    for source in [mine, *sources]:
        write_out(source).wait()
    for copy in sends:
        copy.wait_send()


def gram_scratch(rows):
    return [
        pltpu.VMEM((WIDTH, WIDTH), jnp.float32),
        pltpu.VMEM((WIDTH, WIDTH), jnp.float32),
        pltpu.VMEM((PACKED, TILE), jnp.float32),
        pltpu.VMEM((rows - 1, PACKED // rows, TILE), jnp.float32),
        pltpu.VMEM((PACKED, TILE), jnp.float32),
    ]


def row_sems(rows):
    return [pltpu.SemaphoreType.DMA((rows - 1,))] * 4


ANY_SPEC = pl.BlockSpec(memory_space=pl.ANY)
VMEM_SPEC = pl.BlockSpec(memory_space=pltpu.VMEM)
SMEM_SPEC = pl.BlockSpec(memory_space=pltpu.SMEM)
PANEL_AND_GRAM = (
    jax.ShapeDtypeStruct((ROWS_DEV, WIDTH), jnp.float32),
    jax.ShapeDtypeStruct((PACKED, TILE), jnp.float32),
)


def collect(pairs, rows, unit_rows, channel_scale, seating, unit_counts):
    capacity, columns = unit_rows.shape[2:]
    units = (pairs, capacity, WIDTH)
    return pl.pallas_call(
        functools.partial(collect_kernel, pairs, rows, capacity),
        out_shape=(
            jax.ShapeDtypeStruct(units, jnp.float32),
            jax.ShapeDtypeStruct((PACKED, TILE), jnp.float32),
        ),
        in_specs=[ANY_SPEC, VMEM_SPEC, SMEM_SPEC, SMEM_SPEC],
        out_specs=(ANY_SPEC, VMEM_SPEC),
        scratch_shapes=[
            pltpu.VMEM((capacity, columns), jnp.float32),
            pltpu.VMEM((pairs - 1, capacity, WIDTH), jnp.float32),
            pltpu.VMEM(units, jnp.float32),
            *gram_scratch(rows),
            pltpu.SemaphoreType.DMA((pairs - 1,)),
            pltpu.SemaphoreType.DMA((pairs,)),
            pltpu.SemaphoreType.DMA,
            pltpu.SemaphoreType.DMA((pairs,)),
            *row_sems(rows),
        ],
        compiler_params=pltpu.CompilerParams(
            collective_id=0, has_side_effects=True, vmem_limit_bytes=VMEM_LIMIT
        ),
        name="collect",
    )(unit_rows, channel_scale, seating, unit_counts)


def exchange_kernel(
    pairs, rows,
    old_ref, panel_ref, gram_ref,
    landed, main, cross, packed, parts, total,
    up_send, up_recv, down_send, down_recv, scatter_send, scatter_recv, gather_send, gather_recv,
):
    mine = lax.axis_index("pairs")
    last = pairs - 1
    barrier = pltpu.get_barrier_semaphore()
    signal_peers(barrier, "rows", rows)

    def greet(index):
        pl.semaphore_signal(barrier, inc=1, device_id={"pairs": index}, device_id_type=MESH)

    @pl.when(mine < last)
    def _():
        greet(mine + 1)

    @pl.when(mine > 0)
    def _():
        greet(mine - 1)

    main[...] = jnp.zeros_like(main)
    cross[...] = jnp.zeros_like(cross)
    greeted = jnp.where(mine < last, 1, 0) + jnp.where(mine > 0, 1, 0)
    pl.semaphore_wait(barrier, rows - 1 + greeted)

    size = ROWS_DEV // CHUNKS
    upper, lower = pl.ds(0, BLOCK), pl.ds(BLOCK, BLOCK)

    def up(c, source):
        here = pl.ds(c * size, size)
        return remote(old_ref.at[here, source], landed.at[here, upper], up_send.at[c], up_recv.at[c], "pairs", mine + 1)

    def down(c):
        here = pl.ds(c * size, size)
        return remote(old_ref.at[here, lower], landed.at[here, lower], down_send.at[c], down_recv.at[c], "pairs", mine - 1)

    for c in range(CHUNKS):
        @pl.when(mine == 0)
        def _():
            up(c, lower).start()

        @pl.when((mine > 0) & (mine < last))
        def _():
            up(c, upper).start()

        @pl.when(mine > 0)
        def _():
            down(c).start()

    @pl.when(mine == 0)
    def _():
        landed[:, upper] = old_ref[:, upper]

    @pl.when(mine == last)
    def _():
        landed[:, lower] = old_ref[:, upper]

    for c in range(CHUNKS):
        @pl.when(mine > 0)
        def _():
            up(c, upper).wait_recv()

        @pl.when(mine < last)
        def _():
            down(c).wait_recv()

        add_gram(main, cross, landed[pl.ds(c * size, size), :])
    pack_gram(main, cross, packed)

    def hand_over():
        panel_ref[...] = landed[...]

    sum_over_rows(rows, packed, parts, total, scatter_send, scatter_recv, gather_send, gather_recv, hand_over)
    gram_ref[...] = total[...]
    for c in range(CHUNKS):
        @pl.when(mine < last)
        def _():
            up(c, upper).wait_send()

        @pl.when(mine > 0)
        def _():
            down(c).wait_send()


def exchange(pairs, rows, panel):
    return pl.pallas_call(
        functools.partial(exchange_kernel, pairs, rows),
        out_shape=PANEL_AND_GRAM,
        in_specs=[VMEM_SPEC],
        out_specs=(VMEM_SPEC, VMEM_SPEC),
        scratch_shapes=[
            pltpu.VMEM((ROWS_DEV, WIDTH), jnp.float32),
            *gram_scratch(rows),
            *[pltpu.SemaphoreType.DMA((CHUNKS,))] * 4,
            *row_sems(rows),
        ],
        compiler_params=pltpu.CompilerParams(
            collective_id=1, has_side_effects=True, vmem_limit_bytes=VMEM_LIMIT
        ),
        name="exchange",
    )(panel)


def turn_units_kernel(counts_ref, packed, units_ref, out, units, panel, load_sem, *scratch):
    pairs, room = units.shape[:2]
    load = pltpu.make_async_copy(units_ref, units, load_sem)
    load.start()

    def compact():
        load.wait()
        start = jnp.int32(0)
        groups = room // ALIGN
        lane_row = lax.broadcasted_iota(jnp.int32, (groups + 1, ALIGN, WIDTH), 1)
        for k in range(pairs):
            first = pl.multiple_of(start & -ALIGN, ALIGN)
            shift = start & (ALIGN - 1)
            turned = pltpu.roll(units[k].reshape(groups, ALIGN, WIDTH), shift, 1)
            before = panel[pl.ds(first, ALIGN), :].reshape(1, ALIGN, WIDTH)
            shifted = jnp.where(
                lane_row < shift,
                jnp.concatenate([before, turned], axis=0),
                jnp.concatenate([turned, turned[-1:]], axis=0),
            )
            panel[pl.ds(first, room + ALIGN), :] = shifted.reshape(room + ALIGN, WIDTH)
            start = start + counts_ref[0, k]

    turn_panel(packed, panel, out, compact, *scratch)


def turn_kernel(packed, panel, out, *scratch):
    turn_panel(packed, panel, out, lambda: None, *scratch)


def turn_panel(packed, panel, out, prepare, gram, tangent, square, change):
    diag_row, diag_col = unpack_gram(packed, gram)
    tangent[...] = 0.5 * (
        gram[...] * (diag_row - diag_col) / (2.0 * (diag_col**2 + diag_row**2) + epsilon)
    )
    t_halves = halves(tangent[...])
    square[...] = dot_halves(t_halves, t_halves)
    m_high = square[...].astype(jnp.bfloat16)
    fourth = dot_once(m_high, m_high)
    rest = jnp.sum(fourth * fourth)
    short = rest <= SERIES_BOUND

    @pl.when(short)
    def _():
        first = tangent[...] + square[...]
        second = first + dot_once(first, m_high)
        change[...] = 2.0 * (second + dot_once(second, fourth))

    @pl.when(jnp.logical_not(short))
    def _():
        exact = functools.partial(
            jnp.dot, precision=lax.Precision.HIGHEST, preferred_element_type=jnp.float32
        )
        eye = (
            lax.broadcasted_iota(jnp.int32, (WIDTH, WIDTH), 0)
            == lax.broadcasted_iota(jnp.int32, (WIDTH, WIDTH), 1)
        )
        square[...] = exact(tangent[...], tangent[...])
        bound = jnp.sqrt(jnp.sqrt(jnp.full((1, 1), rest, jnp.float32))) * 1.01
        change[...] = jnp.where(eye, 2.0 / (2.0 + bound), 0.0)

        def newton(step, carry):
            inverse = change[...]
            residual = jnp.where(eye, 1.0, 0.0) - inverse + exact(square[...], inverse)
            change[...] = inverse + exact(inverse, residual)
            return carry

        lax.fori_loop(0, NEWTON_STEPS, newton, 0)
        change[...] = 2.0 * exact(tangent[...] + square[...], change[...])

    prepare()
    d_halves = halves(change[...])
    size = ROWS_DEV // CHUNKS

    def apply(c, carry):
        here = pl.ds(pl.multiple_of(c * size, size), size)
        block = panel[here, :]
        out[here, :] = block + dot_halves(halves(block), d_halves)
        return carry

    lax.fori_loop(0, CHUNKS, apply, 0)


def turn_units(unit_counts, packed, units):
    pairs, room = units.shape[:2]
    return pl.pallas_call(
        turn_units_kernel,
        out_shape=PANEL_AND_GRAM[0],
        in_specs=[SMEM_SPEC, VMEM_SPEC, ANY_SPEC],
        out_specs=VMEM_SPEC,
        scratch_shapes=[
            pltpu.VMEM(units.shape, jnp.float32),
            pltpu.VMEM((ROWS_DEV + room + ALIGN, WIDTH), jnp.float32),
            pltpu.SemaphoreType.DMA,
            *[pltpu.VMEM((WIDTH, WIDTH), jnp.float32)] * 4,
        ],
        compiler_params=pltpu.CompilerParams(vmem_limit_bytes=VMEM_LIMIT),
        name="turn_units",
    )(unit_counts, packed, units)


def turn(packed, panel):
    return pl.pallas_call(
        turn_kernel,
        out_shape=PANEL_AND_GRAM[0],
        in_specs=[VMEM_SPEC, VMEM_SPEC],
        out_specs=VMEM_SPEC,
        scratch_shapes=[pltpu.VMEM((WIDTH, WIDTH), jnp.float32)] * 4,
        compiler_params=pltpu.CompilerParams(vmem_limit_bytes=VMEM_LIMIT),
        name="turn",
    )(packed, panel)


def local(pairs, rows, unit_rows, unit_counts, seating, channel_scale):
    units, gram = collect(pairs, rows, unit_rows, channel_scale[None, :], seating, unit_counts)
    panel = turn_units(unit_counts, gram, units)
    for round_index in range(1, ROUNDS):
        panel, gram = exchange(pairs, rows, panel)
        panel = turn(gram, panel)
    return panel


def solution(mesh):
    return jax.shard_map(
        functools.partial(local, mesh.shape["pairs"], mesh.shape["rows"]),
        mesh=mesh,
        in_specs=(P("rows", "pairs", None, None), P("rows", None), P(), P()),
        out_specs=P("rows", "pairs"),
        check_vma=False,
    )
```
